32 devices in a mesh: section: 2 (over x), shard: 4 (over z), rep: 4 (over y, core).
Axes of the slice: x: 2, y: 2, z: 4, core: 2. Of those that a mesh axis runs over, the one named last changes fastest.
Arguments:
- images: bfloat16 [32, 577, 1024], P(('shard', 'rep')), may hold values from -6 to 6
- cotangent: bfloat16 [32, 577, 1024], P(('shard', 'rep')), may hold values from -6 to 6
- ln1_scale: bfloat16 [2, 1024], P('section', 'shard'), may hold values from 0.5 to 1.5
- ln1_shift: bfloat16 [2, 1024], P('section', 'shard'), may hold values from -2 to 2
- w_qkv: bfloat16 [2, 1024, 3072], P('section', 'shard'), may hold values from -0.1875 to 0.1875
- bias_qv: bfloat16 [2, 2048], P('section', 'shard'), may hold values from -3 to 3
- w_out: bfloat16 [2, 1024, 1024], P('section', 'shard'), may hold values from -2 to 2
- bias_out: bfloat16 [2, 1024], P('section', 'shard'), may hold values from -3 to 3
- ln2_scale: bfloat16 [2, 1024], P('section', 'shard'), may hold values from 0.5 to 1.5
- ln2_shift: bfloat16 [2, 1024], P('section', 'shard'), may hold values from -2 to 2
- w_up: bfloat16 [2, 1024, 4096], P('section', 'shard'), may hold values from -0.1875 to 0.1875
- bias_up: bfloat16 [2, 4096], P('section', 'shard'), may hold values from -3 to 3
- w_down: bfloat16 [2, 4096, 1024], P('section', 'shard'), may hold values from -0.09375 to 0.09375
- bias_down: bfloat16 [2, 1024], P('section', 'shard'), may hold values from -2 to 2
Outputs:
- section_out: bfloat16 [2, 32, 577, 1024], P('section', ('shard', 'rep'))
- grad_in: float32 [2, 32, 577, 1024], P('section', ('shard', 'rep'))
- grad_ln1_scale: float32 [2, 1024], P('section', 'shard')
- grad_ln1_shift: float32 [2, 1024], P('section', 'shard')
- grad_w_qkv: float32 [2, 1024, 3072], P('section', 'shard')
- grad_bias_qv: float32 [2, 2048], P('section', 'shard')
- grad_w_out: float32 [2, 1024, 1024], P('section', 'shard')
- grad_bias_out: float32 [2, 1024], P('section', 'shard')
- grad_ln2_scale: float32 [2, 1024], P('section', 'shard')
- grad_ln2_shift: float32 [2, 1024], P('section', 'shard')
- grad_w_up: float32 [2, 1024, 4096], P('section', 'shard')
- grad_bias_up: float32 [2, 4096], P('section', 'shard')
- grad_w_down: float32 [2, 4096, 1024], P('section', 'shard')
- grad_bias_down: float32 [2, 1024], P('section', 'shard')
The draws below stay inside these ranges and needn't reach their ends.
All inputs are finite; a program needn't handle non-finite values.
Results may differ from the reference program's by a relative error of at most 0.015.
Values may be sent and summed in bfloat16 or wider, within the bound.
No kernel may reach another device: no remote copies, remote signals or barrier semaphores. Data moves between devices by JAX's collectives and lax.ppermute only.
A program may use at most 768 MiB of HBM per device.

```python
import math
import jax
import jax.numpy as jnp
from jax import lax

D = 1024
HEADS = 16
HEAD_DIM = 64
FF = 4096
SEQ = 577
LAYERS = 2
IMAGES = 32


def with_spikes(drawn, own_key, source, target, shards_of, factor):
    def block_of(axis_at):
        return (jnp.arange(drawn.shape[axis_at]) // (drawn.shape[axis_at] // shards_of)).reshape((-1,) + (1,) * (drawn.ndim - 1 - axis_at))

    near = jax.random.permutation(own_key, shards_of)[block_of(target)]
    far = (block_of(target) + shards_of // 2) % shards_of
    return jnp.where((block_of(source) == near) | (block_of(source) == far), factor * drawn, drawn)


def block_levels(stream_key, shape, split, low, high):
    def one(position, blocks):
        draws = jax.random.uniform(jax.random.fold_in(jax.random.fold_in(stream_key, 6), position), (blocks,), jnp.float32, low / len(split), high / len(split))
        return jnp.repeat(jnp.exp(draws), shape[position] // blocks).reshape((-1,) + (1,) * (len(shape) - position - 1))

    gain = one(*split[0])
    for cut in split[1:]:
        gain = gain * one(*cut)
    return gain


def noise(rng, dims, scale, reach, shards=(), kind=jnp.bfloat16):
    values = jax.random.normal(rng, dims, jnp.float32) * scale
    if len(shards) > 0:
        values = block_levels(rng, dims, shards, -0.22, 0.18) * values
    return jnp.clip(values, min=-reach, max=reach).astype(kind)


def heavy_noise(own_key, dims, deviation, most, split, heavy, kind=jnp.bfloat16):
    result = deviation * jax.random.normal(own_key, dims, jnp.float32)
    if split:
        result = result * block_levels(own_key, dims, split, -0.22, 0.18)
    return jnp.clip(with_spikes(result, jax.random.fold_in(own_key, 3), *heavy), -most, most).astype(kind)


def setup_inputs(seed: int = 0) -> dict:
    seeds = jax.random.split(jax.random.key(seed), 15)
    images = heavy_noise(seeds[0], (IMAGES, SEQ, D), 1.0, 6.0, ((0, 16),), (0, 2, 16, 2.0))
    cotangent = noise(seeds[1], (IMAGES, SEQ, D), 1.0, 6.0, ((0, 16),))
    ln1_scale = jnp.clip(1.0 + 0.1 * jax.random.normal(seeds[2], (LAYERS, D), jnp.float32), 0.5, 1.5).astype(jnp.bfloat16)
    ln1_shift = noise(seeds[3], (LAYERS, D), 0.3, 2.0, ((0, 2), (1, 4)))
    w_qkv = noise(seeds[4], (LAYERS, D, 3 * D), D ** -0.5, 0.1875, ((0, 2), (1, 4)))
    bias_qv = noise(seeds[5], (LAYERS, 2 * D), 0.5, 3.0, ((0, 2), (1, 4)))
    w_out = noise(seeds[6], (LAYERS, D, D), (max(D // 128, 2)) ** -0.5, 2.0, ((0, 2), (1, 4)))
    bias_out = noise(seeds[7], (LAYERS, D), 0.5, 3.0, ((0, 2), (1, 4)))
    ln2_scale = jnp.clip(1.0 + 0.1 * jax.random.normal(seeds[8], (LAYERS, D), jnp.float32), 0.5, 1.5).astype(jnp.bfloat16)
    ln2_shift = noise(seeds[9], (LAYERS, D), 0.3, 2.0, ((0, 2), (1, 4)))
    w_up = noise(seeds[10], (LAYERS, D, FF), D ** -0.5, 0.1875, ((0, 2), (1, 4)))
    bias_up = noise(seeds[11], (LAYERS, FF), 0.5, 3.0, ((0, 2), (1, 4)))
    w_down = noise(seeds[12], (LAYERS, FF, D), FF ** -0.5, 0.09375, ((0, 2), (1, 4)))
    bias_down = noise(seeds[13], (LAYERS, D), 0.3, 2.0, ((0, 2), (1, 4)))
    return dict(images=images, cotangent=cotangent, ln1_scale=ln1_scale, ln1_shift=ln1_shift, w_qkv=w_qkv, bias_qv=bias_qv, w_out=w_out, bias_out=bias_out, ln2_scale=ln2_scale, ln2_shift=ln2_shift, w_up=w_up, bias_up=bias_up, w_down=w_down, bias_down=bias_down)


@jax.custom_vjp
def low(v):
    return lax.optimization_barrier(v.astype(jnp.bfloat16)).astype(jnp.float32)

@jax.custom_vjp
def low_back(v):
    return v

def low_keep(v):
    return (low(v), None)

def low_pass(kept, grad):
    return (grad,)

def back_keep(v):
    return (v, None)

def back_low(kept, grad):
    return (low(grad),)
low.defvjp(low_keep, low_pass)
low_back.defvjp(back_keep, back_low)
NORM_EPSILON = 1e-06

def matmul_high(left, right):
    return jnp.dot(left, right, precision=lax.Precision.HIGHEST)

def normed(values, gain_vec, shift_vec):
    average = lax.optimization_barrier(jnp.mean(values, axis=-1, keepdims=True))
    centred = values - average
    spread = lax.optimization_barrier(jnp.mean(centred * centred, axis=-1, keepdims=True))
    return centred * lax.rsqrt(spread + NORM_EPSILON) * gain_vec + shift_vec

def attend(mixed_rows):
    shaped = (SEQ, HEADS, HEAD_DIM)
    queries = mixed_rows[:, :D].reshape(shaped)
    key_rows = mixed_rows[:, D:2 * D].reshape(shaped)
    value_rows = mixed_rows[:, 2 * D:].reshape(shaped)
    scores = jnp.einsum('qhd,khd->hqk', queries, key_rows, precision=lax.Precision.HIGHEST) * HEAD_DIM ** (-0.5)
    scores = low_back(scores)
    attn_prob = low(jax.nn.softmax(scores, axis=-1))
    context = jnp.einsum('hqk,khd->qhd', attn_prob, value_rows, precision=lax.Precision.HIGHEST)
    return context.reshape(SEQ, D)

def layer(rows_in, params):
    gain_one, shift_one, w_mixed, bias_mixed, w_proj, bias_proj, gain_two, shift_two, w_expand, bias_expand, w_reduce, bias_reduce = params
    normed_one = low(normed(rows_in, gain_one, shift_one))
    bias_full = jnp.concatenate([bias_mixed[:D], jnp.zeros((D,), jnp.float32), bias_mixed[D:]])
    mixed_rows = low(low_back(matmul_high(normed_one, w_mixed) + bias_full))
    context = lax.map(jax.checkpoint(attend), mixed_rows.reshape(-1, SEQ, 3 * D)).reshape(-1, D)
    context = low(low_back(context))
    after_attn = rows_in + low_back(matmul_high(context, w_proj) + bias_proj)
    normed_two = low(normed(after_attn, gain_two, shift_two))
    hidden_pre = low_back(matmul_high(normed_two, w_expand) + bias_expand)
    hidden = low(jax.nn.gelu(hidden_pre, approximate=False))
    return after_attn + low_back(matmul_high(hidden, w_reduce) + bias_reduce)

def forward(params, image_block, delta_rows):
    hidden_rows = image_block.reshape(-1, D)
    layer_outs = []
    for layer_at in range(LAYERS):
        if layer_at > 0:
            hidden_rows = low(low_back(hidden_rows + delta_rows[layer_at - 1].reshape(-1, D)))
        hidden_rows = layer(hidden_rows, tuple((member[layer_at] for member in params)))
        layer_outs.append(low(hidden_rows).reshape(-1, SEQ, D))
    return jnp.stack(layer_outs, axis=0)

def reference(images, cotangent, ln1_scale, ln1_shift, w_qkv, bias_qv, w_out, bias_out, ln2_scale, ln2_shift, w_up, bias_up, w_down, bias_down):
    params = tuple((member.astype(jnp.float32) for member in (ln1_scale, ln1_shift, w_qkv, bias_qv, w_out, bias_out, ln2_scale, ln2_shift, w_up, bias_up, w_down, bias_down)))
    group_size = math.gcd(IMAGES, 4)
    group_count = IMAGES // group_size
    image_groups = images.astype(jnp.float32).reshape(group_count, group_size, SEQ, D)
    delta_rows = jnp.zeros((group_count, LAYERS - 1, group_size, SEQ, D), jnp.float32)

    def whole_model(params, image_groups, delta_rows):

        def one_group(item_pair):
            return forward(params, item_pair[0], item_pair[1])
        return lax.map(jax.checkpoint(one_group), (image_groups, delta_rows))
    stacked, pullback = jax.vjp(whole_model, params, image_groups, delta_rows)
    seed_grad = jnp.zeros_like(stacked).at[:, LAYERS - 1].set(cotangent.astype(jnp.float32).reshape(group_count, group_size, SEQ, D))
    gradients, image_grad, delta_grad = pullback(seed_grad)
    section_out = jnp.transpose(stacked, (1, 0, 2, 3, 4)).reshape(LAYERS, IMAGES, SEQ, D).astype(jnp.bfloat16)
    later_grad = jnp.transpose(delta_grad, (1, 0, 2, 3, 4)).reshape(LAYERS - 1, IMAGES, SEQ, D)
    grad_in = jnp.concatenate([image_grad.reshape(1, IMAGES, SEQ, D), later_grad], axis=0)
    return (section_out, grad_in, gradients[0], gradients[1], gradients[2], gradients[3], gradients[4], gradients[5], gradients[6], gradients[7], gradients[8], gradients[9], gradients[10], gradients[11])
```

```python
from functools import partial

import jax
import jax.numpy as jnp
from jax import lax
from jax.experimental import pallas as pl
from jax.experimental.pallas import tpu as pltpu
from jax.sharding import PartitionSpec as P

HEAD_DIM = 64
CORES = 2
NORM_EPSILON = 1e-06
LOG2E = 1.4426950408889634
VMEM_BYTES = 56 * 1024 * 1024
F32 = jnp.float32
BF16 = jnp.bfloat16


def nn(left, right):
    return jnp.dot(left, right, preferred_element_type=F32)


def nt(left, right):
    return lax.dot_general(left, right, (((1,), (1,)), ((), ())), preferred_element_type=F32)


def tn(left, right):
    return lax.dot_general(left, right, (((0,), (0,)), ((), ())), preferred_element_type=F32)


def unit(values):
    centred = values - jnp.mean(values, axis=-1, keepdims=True)
    inv = lax.rsqrt(jnp.mean(centred * centred, axis=-1, keepdims=True) + NORM_EPSILON)
    return centred * inv, inv


def norm_back(grad, unit_rows, inv, gain):
    e = grad * gain
    return inv * (
        e
        - jnp.mean(e, axis=-1, keepdims=True)
        - unit_rows * jnp.mean(e * unit_rows, axis=-1, keepdims=True)
    )


def col_sum(values):
    return jnp.sum(values.astype(F32), axis=0, keepdims=True)


def gelu_parts(x):
    z = jnp.abs(x) * 0.7071067811865476
    t = 1.0 / (1.0 + 0.3275911 * z)
    e = jnp.exp2(x * x * (-0.5 * LOG2E))
    poly = t * (
        0.254829592
        + t * (-0.284496736 + t * (1.421413741 + t * (-1.453152027 + t * 1.061405429)))
    )
    tail = 0.5 * poly * e
    cdf = jnp.where(x >= 0, 1.0 - tail, tail)
    return x * cdf, cdf + x * (e * 0.3989422804014327)


def spec(shape, index):
    return pl.BlockSpec(shape, index)


def fixed(shape, at=None):
    at = (0,) * len(shape) if at is None else at
    return pl.BlockSpec(shape, lambda *_: at)


def call(kernel, name, grid, ins, outs, scratch=(), scalars=None, prev=None, flops=0):
    arrays = [a for a, _ in ins]
    in_specs = [s for _, s in ins]
    body = kernel
    aliases = {}
    n_scalar = 0 if scalars is None else 1
    if prev is not None:
        count = len(ins)
        held = [(i, p) for i, p in enumerate(prev) if p is not None]
        for k, (i, p) in enumerate(held):
            aliases[n_scalar + count + k] = i
            arrays.append(p)
            in_specs.append(pl.BlockSpec(memory_space=pl.ANY))

        def body(*refs):
            kernel(*refs[: n_scalar + count], *refs[n_scalar + count + len(held) :])

    moved = sum(a.size * a.dtype.itemsize for a, _ in ins)
    cost = pl.CostEstimate(flops=int(flops), bytes_accessed=int(moved), transcendentals=0)
    params = pltpu.CompilerParams(
        dimension_semantics=("arbitrary",) * len(grid), vmem_limit_bytes=VMEM_BYTES
    )
    out_shape = [jax.ShapeDtypeStruct(s, d) for s, d, _ in outs]
    out_specs = [s for _, _, s in outs]
    if scalars is None:
        f = pl.pallas_call(
            body,
            grid=grid,
            in_specs=in_specs,
            out_specs=out_specs,
            out_shape=out_shape,
            scratch_shapes=list(scratch),
            input_output_aliases=aliases,
            compiler_params=params,
            cost_estimate=cost,
            name=name,
        )
        return f(*arrays)
    f = pl.pallas_call(
        body,
        grid_spec=pltpu.PrefetchScalarGridSpec(
            num_scalar_prefetch=1,
            grid=grid,
            in_specs=in_specs,
            out_specs=out_specs,
            scratch_shapes=list(scratch),
        ),
        out_shape=out_shape,
        input_output_aliases=aliases,
        compiler_params=params,
        cost_estimate=cost,
        name=name,
    )
    return f(scalars, *arrays)


def ln_qkv_kernel(x_ref, g_ref, b_ref, w_ref, bq_ref, xb_ref, n1_ref, o_ref):
    @pl.when(pl.program_id(0) == 0)
    def _():
        x = x_ref[...]
        xb_ref[...] = x
        u, _ = unit(x.astype(F32))
        n1_ref[...] = (u * g_ref[...].astype(F32) + b_ref[...].astype(F32)).astype(BF16)

    o_ref[...] = (nn(n1_ref[...], w_ref[...]) + bq_ref[...].astype(F32)).astype(BF16)


def ln_qkv(x, gain, shift, w, bias, slot, slots, prev):
    s, d = x.shape
    n = w.shape[1]
    t = 1024
    return call(
        ln_qkv_kernel,
        "ln_qkv",
        (n // t,),
        [
            (x, fixed((s, d))),
            (gain, fixed((1, d))),
            (shift, fixed((1, d))),
            (w, spec((d, t), lambda j: (0, j))),
            (bias, spec((1, t), lambda j: (0, j))),
        ],
        [
            ((slots, s, d), BF16, fixed((None, s, d), (slot, 0, 0))),
            ((slots, s, d), BF16, fixed((None, s, d), (slot, 0, 0))),
            ((slots, s, n), BF16, spec((None, s, t), lambda j: (slot, 0, j))),
        ],
        prev=prev,
        flops=2 * s * d * n,
    )


def attn_kernel(q_ref, k_ref, v_ref, o_ref, l_ref):
    scale = LOG2E * HEAD_DIM**-0.5
    outs = []
    logs = []
    for h in range(2):
        at = slice(h * HEAD_DIM, (h + 1) * HEAD_DIM)
        scores = nt(q_ref[:, at], k_ref[:, at])
        top = jnp.max(scores, axis=-1, keepdims=True)
        p = jnp.exp2((scores - top) * scale)
        total = jnp.sum(p, axis=-1, keepdims=True)
        outs.append((nn(p.astype(BF16), v_ref[:, at]) * (1.0 / total)).astype(BF16))
        logs.append(top * scale + jnp.log2(total))
    o_ref[...] = jnp.concatenate(outs, axis=1)
    l_ref[...] = jnp.concatenate(logs, axis=1)


def attn(qkv, slot, prev):
    slots, s, n = qkv.shape
    d = n // 3
    pairs = d // 128

    def block(part):
        return spec((None, s, 128), lambda j: (slot, 0, j + part * pairs))

    return call(
        attn_kernel,
        "attn",
        (pairs,),
        [(qkv, block(0)), (qkv, block(1)), (qkv, block(2))],
        [
            ((slots, s, d), BF16, block(0)),
            ((slots, pairs, s, 2), F32, spec((None, None, s, 2), lambda j: (slot, j, 0, 0))),
        ],
        prev=prev,
        flops=4 * s * s * d * 3,
    )


def out_ln_kernel(c_ref, x_ref, w_ref, bo_ref, g_ref, b_ref, a_ref, n_ref):
    a = x_ref[...].astype(F32) + (nn(c_ref[...], w_ref[...]) + bo_ref[...].astype(F32))
    a_ref[...] = a
    u, _ = unit(a)
    n_ref[...] = (u * g_ref[...].astype(F32) + b_ref[...].astype(F32)).astype(BF16)


def out_ln(ctx, x, w, bias, gain, shift, slot, prev):
    slots, s, d = ctx.shape
    at = fixed((None, s, d), (slot, 0, 0))
    vec = fixed((1, d))
    return call(
        out_ln_kernel,
        "out_ln",
        (1,),
        [(ctx, at), (x, fixed((s, d))), (w, fixed((d, d))), (bias, vec), (gain, vec), (shift, vec)],
        [((slots, s, d), F32, at), ((slots, s, d), BF16, at)],
        prev=prev,
        flops=2 * s * d * d,
    )


def up_gelu_kernel(n_ref, w_ref, b_ref, h_ref, gp_ref):
    h, gp = gelu_parts(nn(n_ref[...], w_ref[...]) + b_ref[...].astype(F32))
    h_ref[...] = h.astype(BF16)
    gp_ref[...] = gp.astype(BF16)


def up_gelu(n2, w, bias, slot, prev):
    slots, s, d = n2.shape
    n = w.shape[1]
    t = 512
    out = ((slots, s, n), BF16, spec((None, s, t), lambda j: (slot, 0, j)))
    return call(
        up_gelu_kernel,
        "up_gelu",
        (n // t,),
        [
            (n2, fixed((None, s, d), (slot, 0, 0))),
            (w, spec((d, t), lambda j: (0, j))),
            (bias, spec((1, t), lambda j: (0, j))),
        ],
        [out, out],
        prev=prev,
        flops=3 * s * d * n,
    )


def down_kernel(h_ref, w_ref, a_ref, b_ref, o_ref, acc):
    j = pl.program_id(0)

    @pl.when(j == 0)
    def _():
        acc[...] = a_ref[...] + b_ref[...].astype(F32)

    acc[...] += nn(h_ref[...], w_ref[...])

    @pl.when(j == pl.num_programs(0) - 1)
    def _():
        o_ref[...] = acc[...].astype(BF16)


def down(hidden, w, after, bias, slot):
    _, s, n = hidden.shape
    d = w.shape[1]
    t = 1024
    return call(
        down_kernel,
        "down",
        (n // t,),
        [
            (hidden, spec((None, s, t), lambda j: (slot, 0, j))),
            (w, spec((t, d), lambda j: (j, 0))),
            (after, fixed((None, s, d), (slot, 0, 0))),
            (bias, fixed((1, d))),
        ],
        [((s, d), BF16, fixed((s, d)))],
        scratch=[pltpu.VMEM((s, d), F32)],
        flops=2 * s * d * n,
    )[0]


def mlp_back_kernel(
    at_ref, g_ref, gp_ref, wd_ref, wu_ref, a_ref, gain_ref, wo_ref,
    gd_ref, gu_ref, ga_ref, gt_ref, gc_ref, dbu_ref, sm_ref, acc,
):
    j = pl.program_id(0)
    gu = (nt(g_ref[...], wd_ref[...]) * gp_ref[...].astype(F32)).astype(BF16)
    gu_ref[...] = gu
    dbu_ref[...] = col_sum(gu)

    @pl.when(j == 0)
    def _():
        acc[...] = jnp.zeros_like(acc)

    acc[...] += nt(gu, wu_ref[...])

    @pl.when(j == pl.num_programs(0) - 1)
    def _():
        gn = acc[...]
        u, r = unit(a_ref[...])
        gd_ref[...] = g_ref[...]
        g = g_ref[...].astype(F32)
        ga = g + norm_back(gn, u, r, gain_ref[...].astype(F32))
        ga_ref[...] = ga
        gt = ga.astype(BF16)
        gt_ref[...] = gt
        gc_ref[...] = nt(gt, wo_ref[...]).astype(BF16)
        sm_ref[0:1, :] = col_sum(gn * u)
        sm_ref[1:2, :] = col_sum(gn)
        sm_ref[2:3, :] = col_sum(g)
        sm_ref[3:4, :] = col_sum(gt)


def mlp_back(at, g, gp, wd, wu, after, gain, wo, slot, slots, prev):
    s, d = g.shape
    n = gp.shape[2]
    t = 512
    row = fixed((None, s, d), (slot, 0, 0))
    return call(
        mlp_back_kernel,
        "mlp_back",
        (n // t,),
        [
            (g, fixed((s, d))),
            (gp, spec((None, s, t), lambda j, r: (r[0], 0, j))),
            (wd, spec((t, d), lambda j, r: (j, 0))),
            (wu, spec((d, t), lambda j, r: (0, j))),
            (after, spec((None, s, d), lambda j, r: (r[0], 0, 0))),
            (gain, fixed((1, d))),
            (wo, fixed((d, d))),
        ],
        [
            ((slots, s, d), BF16, row),
            ((slots, s, n), BF16, spec((None, s, t), lambda j, r: (slot, 0, j))),
            ((s, d), F32, fixed((s, d))),
            ((slots, s, d), BF16, row),
            ((s, d), BF16, fixed((s, d))),
            ((slots, 1, n), F32, spec((None, 1, t), lambda j, r: (slot, 0, j))),
            ((slots, 4, d), F32, fixed((None, 4, d), (slot, 0, 0))),
        ],
        scratch=[pltpu.VMEM((s, d), F32)],
        scalars=at,
        prev=prev,
        flops=4 * s * d * n + 2 * s * d * d,
    )


def attn_back_kernel(at_ref, q_ref, k_ref, v_ref, do_ref, l_ref, o_ref):
    scale = LOG2E * HEAD_DIM**-0.5
    d = o_ref.shape[1] // 3
    dqs, dks, dvs = [], [], []
    for h in range(2):
        at = slice(h * HEAD_DIM, (h + 1) * HEAD_DIM)
        q, k, v, do = q_ref[:, at], k_ref[:, at], v_ref[:, at], do_ref[:, at]
        p = jnp.exp2(nt(q, k) * scale - l_ref[:, h : h + 1])
        dp = nt(do, v)
        dvs.append(tn(p.astype(BF16), do).astype(BF16))
        pdp = p * dp
        ds = (pdp - p * jnp.sum(pdp, axis=-1, keepdims=True)).astype(BF16)
        dqs.append((nn(ds, k) * HEAD_DIM**-0.5).astype(BF16))
        dks.append((tn(ds, q) * HEAD_DIM**-0.5).astype(BF16))
    j = pl.program_id(0)
    for part, pieces in enumerate((dqs, dks, dvs)):
        first = pl.multiple_of(part * d + j * 128, 128)
        o_ref[:, pl.ds(first, 128)] = jnp.concatenate(pieces, axis=1)


def attn_back(at, qkv, gc, logs, slot, slots, prev):
    _, s, n = qkv.shape
    d = n // 3
    pairs = d // 128

    def block(part):
        return spec((None, s, 128), lambda j, r: (r[0], 0, j + part * pairs))

    return call(
        attn_back_kernel,
        "attn_back",
        (pairs,),
        [
            (qkv, block(0)),
            (qkv, block(1)),
            (qkv, block(2)),
            (gc, spec((s, 128), lambda j, r: (0, j))),
            (logs, spec((None, None, s, 2), lambda j, r: (r[0], j, 0, 0))),
        ],
        [((slots, s, n), BF16, fixed((None, s, n), (slot, 0, 0)))],
        scalars=at,
        prev=prev,
        flops=10 * s * s * d * 3,
    )[0]


def qkv_back_kernel(at_ref, g_ref, w_ref, x_ref, ga_ref, gain_ref, o_ref, ob_ref, sm_ref):
    d = x_ref.shape[1]
    gn = nt(g_ref[...], w_ref[...])
    u, r = unit(x_ref[...].astype(F32))
    out = ga_ref[...] + norm_back(gn, u, r, gain_ref[...].astype(F32))
    o_ref[...] = out
    ob_ref[...] = out.astype(BF16)
    sm_ref[0:1, :] = col_sum(gn * u)
    sm_ref[1:2, :] = col_sum(gn)
    sm_ref[2:3, :] = col_sum(g_ref[:, 0:d])
    sm_ref[3:4, :] = col_sum(g_ref[:, 2 * d : 3 * d])


def qkv_back(at, gqkv, w, xb, ga, gain, slot, prev):
    slots, s, n = gqkv.shape
    d = n // 3
    return call(
        qkv_back_kernel,
        "qkv_back",
        (1,),
        [
            (gqkv, fixed((None, s, n), (slot, 0, 0))),
            (w, fixed((d, n))),
            (xb, spec((None, s, d), lambda j, r: (r[0], 0, 0))),
            (ga, fixed((s, d))),
            (gain, fixed((1, d))),
        ],
        [
            ((s, d), F32, fixed((s, d))),
            ((s, d), BF16, fixed((s, d))),
            ((slots, 4, d), F32, fixed((None, 4, d), (slot, 0, 0))),
        ],
        scalars=at,
        prev=prev,
        flops=2 * s * d * n,
    )


def weight_grad_kernel(at_ref, a_ref, k0_ref, k1_ref, s0_ref, s1_ref, keep_ref, send_ref):
    a0, a1 = a_ref[0], a_ref[1]
    keep_ref[...] = (tn(a0, k0_ref[...]) + tn(a1, k1_ref[...])).astype(BF16)
    send_ref[...] = (tn(a0, s0_ref[...]) + tn(a1, s1_ref[...])).astype(BF16)


def weight_grad(at, left, right, owners, replicas, name):
    _, s, m = left.shape
    n = right.shape[2]
    chips = replicas // CORES
    rows, cols = m // owners, n // replicas

    def col(image, other):
        def index(z, y, r):
            core = 1 - r[2] if other else r[2]
            return (r[1] + image, 0, y * CORES + core)

        return spec((None, s, cols), index)

    out = (
        (owners, chips, rows, cols),
        BF16,
        spec((None, None, rows, cols), lambda z, y, r: (z, y, 0, 0)),
    )
    return call(
        weight_grad_kernel,
        name,
        (owners, chips),
        [
            (left, spec((2, s, rows), lambda z, y, r: (r[0], 0, z))),
            (right, col(0, False)),
            (right, col(1, False)),
            (right, col(0, True)),
            (right, col(1, True)),
        ],
        [out, out],
        scalars=at,
        flops=4 * s * m * n,
    )


class Place:
    def __init__(self):
        self.owners = lax.axis_size("shard")
        self.replicas = lax.axis_size("rep")
        self.chips = self.replicas // CORES
        self.z = lax.axis_index("shard")
        rep = lax.axis_index("rep")
        self.rep = rep
        self.y = rep // CORES
        self.core = rep % CORES

    def ring_z(self, block):
        n = self.owners
        return lax.ppermute(block, "shard", [(i, (i + 1) % n) for i in range(n)])

    def ring_y(self, block):
        n = self.chips
        route = [
            (y * CORES + c, ((y + 1) % n) * CORES + c) for y in range(n) for c in range(CORES)
        ]
        return lax.ppermute(block, "rep", route)

    def swap_core(self, block):
        route = [(i, i ^ 1) for i in range(self.replicas)]
        return lax.ppermute(block, "rep", route)


def assemble_kernel(count, plan, at_ref, *refs):
    pieces, out_ref, sems = refs[:count], refs[count], refs[count + 1]
    z, y, c = at_ref[0], at_ref[1], at_ref[2]
    owners, replicas, rows, _ = out_ref.shape
    chips = replicas // CORES
    copies = []
    for i, (piece, (s, t, other)) in enumerate(zip(pieces, plan)):
        if s == 0:
            target = out_ref.at[z]
        else:
            core = 1 - c if other else c
            quarter = lax.rem(y - t + chips, chips) * CORES + core
            target = out_ref.at[lax.rem(z - s + owners, owners), quarter]
        copies.append(pltpu.make_async_copy(piece, target, sems.at[i]))
    for copy in copies:
        copy.start()
    for copy in copies:
        copy.wait()


def gather_weight(place, w):
    rows, n = w.shape
    part = rows // place.replicas
    mine = lax.dynamic_slice_in_dim(w, place.rep * part, part, 0)
    pieces = [w.reshape(place.replicas, part, n)]
    plan = [(0, 0, False)]
    ring = mine
    for s in range(1, place.owners):
        ring = place.ring_z(ring)
        held = ring
        for t in range(place.chips):
            if t > 0:
                held = place.ring_y(held)
            pieces.append(held)
            plan.append((s, t, False))
            pieces.append(place.swap_core(held))
            plan.append((s, t, True))
    count = len(pieces)
    at = jnp.stack([place.z, place.y, place.core]).astype(jnp.int32)
    out = pl.pallas_call(
        partial(assemble_kernel, count, plan),
        in_specs=[pl.BlockSpec(memory_space=pltpu.SMEM)]
        + [pl.BlockSpec(memory_space=pl.ANY)] * count,
        out_specs=pl.BlockSpec(memory_space=pltpu.VMEM),
        out_shape=jax.ShapeDtypeStruct((place.owners, place.replicas, part, n), w.dtype),
        scratch_shapes=[pltpu.SemaphoreType.DMA((count,))],
        compiler_params=pltpu.CompilerParams(vmem_limit_bytes=VMEM_BYTES),
        cost_estimate=pl.CostEstimate(
            flops=0, bytes_accessed=4 * place.owners * w.size, transcendentals=0
        ),
        name="assemble",
    )(at, *pieces)
    return out.reshape(place.owners * rows, n)


def add(left, right):
    return (left.astype(F32) + right.astype(F32)).astype(BF16)


def pick(holder, index, axis):
    return lax.dynamic_index_in_dim(holder, index, axis, keepdims=False)


def reduce_weight(place, keep, send):
    held = add(keep, place.swap_core(send))
    chips, owners = place.chips, place.owners
    total = pick(held, lax.rem(place.y + chips - 1, chips), 1)
    for step in range(1, chips):
        total = add(
            place.ring_y(total), pick(held, lax.rem(place.y + 2 * chips - 1 - step, chips), 1)
        )
    held = total
    total = pick(held, lax.rem(place.z + owners - 1, owners), 0)
    for step in range(1, owners):
        total = add(
            place.ring_z(total), pick(held, lax.rem(place.z + 2 * owners - 1 - step, owners), 0)
        )
    whole = lax.all_gather(total, "rep", axis=0)
    rows, cols = total.shape
    return jnp.transpose(whole, (1, 0, 2)).reshape(1, rows, place.replicas * cols).astype(F32)


def per_device(
    images, cotangent, ln1_scale, ln1_shift, w_qkv, bias_qv, w_out, bias_out,
    ln2_scale, ln2_shift, w_up, bias_up, w_down, bias_down,
):
    place = Place()
    section = lax.axis_index("section")
    first = section == 0
    _, s, d = images.shape

    vectors = (
        ln1_scale, ln1_shift, bias_qv, bias_out, ln2_scale, ln2_shift, bias_up, bias_down
    )
    widths = [v.shape[1] for v in vectors]
    packed = lax.all_gather(jnp.concatenate(vectors, axis=1)[0], "shard", axis=0)
    whole = []
    start = 0
    for width in widths:
        whole.append(packed[:, start : start + width].reshape(1, -1))
        start += width
    gain1, shift1, bias_two, bias_o, gain2, shift2, bias_u, bias_d = whole
    bias_mixed = jnp.concatenate(
        [bias_two[:, :d], jnp.zeros((1, d), BF16), bias_two[:, d:]], axis=1
    )
    wq = gather_weight(place, w_qkv[0])
    wo = gather_weight(place, w_out[0])
    wu = gather_weight(place, w_up[0])
    wd = gather_weight(place, w_down[0])

    slots = 4
    xb = n1 = qkv = ctx = logs = after = n2 = hidden = gp = None

    def send_on(block):
        return lax.ppermute(block, "section", [(0, 1)])

    def send_back(block):
        return lax.ppermute(block, "section", [(1, 0)])

    outs = []
    arrived = []
    for slot in range(slots):
        x = images[slot] if slot < 2 else arrived[slot - 2]
        xb, n1, qkv = ln_qkv(x, gain1, shift1, wq, bias_mixed, slot, slots, (xb, n1, qkv))
        ctx, logs = attn(qkv, slot, (ctx, logs))
        after, n2 = out_ln(ctx, x, wo, bias_o, gain2, shift2, slot, (after, n2))
        hidden, gp = up_gelu(n2, wu, bias_u, slot, (hidden, gp))
        out = down(hidden, wd, after, bias_d, slot)
        outs.append(out)
        if slot < 2:
            arrived.append(send_on(out))
    section_out = jnp.where(first, jnp.stack(outs[:2]), jnp.stack(outs[2:]))

    gslots = 3
    gd = gu = gt = gqkv = dbu = sm2 = sm1 = None
    upstream = cotangent[0]
    grads = []
    for slot in range(gslots):
        source = [jnp.full((), 2), jnp.where(first, 0, 3), jnp.full((), 1)][slot]
        at = source.astype(jnp.int32).reshape(1)
        gd, gu, ga, gt, gc, dbu, sm2 = mlp_back(
            at, upstream, gp, wd, wu, after, gain2, wo, slot, gslots,
            (gd, gu, None, gt, None, dbu, sm2),
        )
        gqkv = attn_back(at, qkv, gc, logs, slot, gslots, (gqkv,))
        grad, low, sm1 = qkv_back(at, gqkv, wq, xb, ga, gain1, slot, (None, None, sm1))
        grads.append((grad, low))
        if slot == 0:
            upstream = jnp.where(first, send_back(low), cotangent[1])
        elif slot == 1:
            upstream = send_back(low)

    low = [g[1].astype(F32) for g in grads]
    grad_in = jnp.where(
        first, jnp.stack([grads[1][0], grads[2][0]]), jnp.stack([low[0], low[1]])
    )
    at = jnp.stack([section, 1 - section, place.core]).astype(jnp.int32)

    def products(left, right, name):
        return weight_grad(at, left, right, place.owners, place.replicas, name)

    gw_down = reduce_weight(place, *products(hidden, gd, "dw_down"))
    gw_up = reduce_weight(place, *products(n2, gu, "dw_up"))
    gw_out = reduce_weight(place, *products(ctx, gt, "dw_out"))
    gw_qkv = reduce_weight(place, *products(n1, gqkv, "dw_qkv"))

    def own(holder):
        pair = lax.dynamic_slice_in_dim(holder, 1 - section, 2, 0)
        return jnp.sum(pair, axis=0)

    sm1, sm2, dbu = own(sm1), own(sm2), own(dbu)
    smalls = (
        sm1[0:1], sm1[1:2], jnp.concatenate([sm1[2:3], sm1[3:4]], axis=1), sm2[3:4],
        sm2[0:1], sm2[1:2], dbu, sm2[2:3],
    )
    table = jnp.concatenate([v.reshape(place.owners, -1) for v in smalls], axis=1)
    table = lax.psum(table, ("shard", "rep"))
    mine = lax.dynamic_slice_in_dim(table, place.z, 1, 0)
    shares = []
    start = 0
    for width in widths:
        shares.append(mine[:, start : start + width])
        start += width
    (g_ln1s, g_ln1b, g_bqv, g_bo, g_ln2s, g_ln2b, g_bu, g_bd) = shares
    return (
        section_out[None], grad_in[None], g_ln1s, g_ln1b, gw_qkv, g_bqv, gw_out, g_bo,
        g_ln2s, g_ln2b, gw_up, g_bu, gw_down, g_bd,
    )


def solution(mesh):
    batch = P(("shard", "rep"), None, None)
    layers = P("section", ("shard", "rep"), None, None)
    vec = P("section", "shard")
    mat = P("section", "shard", None)
    in_specs = (
        batch, batch, vec, vec, mat, vec, mat, vec, vec, vec, mat, vec, mat, vec
    )
    out_specs = (
        layers, layers, vec, vec, mat, vec, mat, vec, vec, vec, mat, vec, mat, vec
    )
    return jax.shard_map(
        per_device, mesh=mesh, in_specs=in_specs, out_specs=out_specs, check_vma=False
    )
```

```python
from functools import partial

import jax
import jax.numpy as jnp
from jax import lax
from jax.experimental import pallas as pl
from jax.experimental.pallas import tpu as pltpu
from jax.sharding import PartitionSpec as P

HEAD_DIM = 64
CORES = 2
NORM_EPSILON = 1e-06
LOG2E = 1.4426950408889634
VMEM_BYTES = 56 * 1024 * 1024
F32 = jnp.float32
BF16 = jnp.bfloat16
COST = 1


def nn(left, right):
    return jnp.dot(left, right, preferred_element_type=F32)


def nt(left, right):
    return lax.dot_general(left, right, (((1,), (1,)), ((), ())), preferred_element_type=F32)


def tn(left, right):
    return lax.dot_general(left, right, (((0,), (0,)), ((), ())), preferred_element_type=F32)


def unit(values):
    centred = values - jnp.mean(values, axis=-1, keepdims=True)
    inv = lax.rsqrt(jnp.mean(centred * centred, axis=-1, keepdims=True) + NORM_EPSILON)
    return centred * inv, inv


def norm_back(grad, unit_rows, inv, gain):
    e = grad * gain
    return inv * (
        e
        - jnp.mean(e, axis=-1, keepdims=True)
        - unit_rows * jnp.mean(e * unit_rows, axis=-1, keepdims=True)
    )


def col_sum(values):
    return jnp.sum(values.astype(F32), axis=0, keepdims=True)


def gelu_parts(x):
    z = jnp.abs(x) * 0.7071067811865476
    t = pl.reciprocal(1.0 + 0.3275911 * z, approx=True)
    e = jnp.exp2(x * x * (-0.5 * LOG2E))
    poly = t * (
        0.254829592
        + t * (-0.284496736 + t * (1.421413741 + t * (-1.453152027 + t * 1.061405429)))
    )
    tail = 0.5 * poly * e
    cdf = jnp.where(x >= 0, 1.0 - tail, tail)
    return x * cdf, cdf + x * (e * 0.3989422804014327)


def spec(shape, index):
    return pl.BlockSpec(shape, index)


def fixed(shape, at=None):
    at = (0,) * len(shape) if at is None else at
    return pl.BlockSpec(shape, lambda *_: at)


def call(kernel, name, grid, ins, outs, scratch=(), scalars=None, prev=None, wait=(), flops=0):
    arrays = [a for a, _ in ins]
    in_specs = [s for _, s in ins]
    body = kernel
    if len(wait) > 0:
        read, prev = len(ins) + (scalars is not None), prev or [None] * len(outs)
        arrays += list(wait)
        in_specs += [pl.BlockSpec(memory_space=pl.ANY)] * len(wait)
        ins = list(ins) + [(w, None) for w in wait]
        inner = kernel

        def kernel(*refs):
            inner(*refs[:read], *refs[read + len(wait) :])

        body = kernel
    aliases = {}
    n_scalar = 0 if scalars is None else 1
    if prev is not None:
        count = len(ins)
        held = [(i, p) for i, p in enumerate(prev) if p is not None]
        for k, (i, p) in enumerate(held):
            aliases[n_scalar + count + k] = i
            arrays.append(p)
            in_specs.append(pl.BlockSpec(memory_space=pl.ANY))

        def body(*refs):
            kernel(*refs[: n_scalar + count], *refs[n_scalar + count + len(held) :])

    cost = pl.CostEstimate(flops=int(flops * COST), bytes_accessed=0, transcendentals=0)
    params = pltpu.CompilerParams(
        dimension_semantics=("arbitrary",) * len(grid), vmem_limit_bytes=VMEM_BYTES
    )
    out_shape = [jax.ShapeDtypeStruct(s, d) for s, d, _ in outs]
    out_specs = [s for _, _, s in outs]
    if scalars is None:
        f = pl.pallas_call(
            body,
            grid=grid,
            in_specs=in_specs,
            out_specs=out_specs,
            out_shape=out_shape,
            scratch_shapes=list(scratch),
            input_output_aliases=aliases,
            compiler_params=params,
            cost_estimate=cost,
            name=name,
        )
        return f(*arrays)
    f = pl.pallas_call(
        body,
        grid_spec=pltpu.PrefetchScalarGridSpec(
            num_scalar_prefetch=1,
            grid=grid,
            in_specs=in_specs,
            out_specs=out_specs,
            scratch_shapes=list(scratch),
        ),
        out_shape=out_shape,
        input_output_aliases=aliases,
        compiler_params=params,
        cost_estimate=cost,
        name=name,
    )
    return f(scalars, *arrays)


def ln_qkv_kernel(x_ref, g_ref, b_ref, w_ref, bq_ref, xb_ref, n1_ref, o_ref):
    @pl.when(pl.program_id(0) == 0)
    def _():
        x = x_ref[...]
        xb_ref[...] = x
        u, _ = unit(x.astype(F32))
        n1_ref[...] = (u * g_ref[...].astype(F32) + b_ref[...].astype(F32)).astype(BF16)

    o_ref[...] = (nn(n1_ref[...], w_ref[...]) + bq_ref[...].astype(F32)).astype(BF16)


def ln_qkv(x, gain, shift, w, bias, slot, slots, prev):
    s, d = x.shape
    n = bias.shape[1]
    t = 1024
    return call(
        ln_qkv_kernel,
        "ln_qkv",
        (n // t,),
        [
            (x, fixed((s, d))),
            (gain, fixed((1, d))),
            (shift, fixed((1, d))),
            (w, spec((d, t), lambda j: (0, j))),
            (bias, spec((1, t), lambda j: (0, j))),
        ],
        [
            ((slots, s, d), BF16, fixed((None, s, d), (slot, 0, 0))),
            ((slots, s, d), BF16, fixed((None, s, d), (slot, 0, 0))),
            ((slots, s, n), BF16, spec((None, s, t), lambda j: (slot, 0, j))),
        ],
        prev=prev,
        flops=2 * s * d * n,
    )


def head_slices(count):
    return [slice(h * HEAD_DIM, (h + 1) * HEAD_DIM) for h in range(count)]


def attn_kernel(q_ref, k_ref, v_ref, o_ref, l_ref):
    scale = LOG2E * HEAD_DIM**-0.5
    heads = head_slices(l_ref.shape[0])
    values = v_ref[...].T
    scores = [nt(k_ref[:, at], q_ref[:, at]) for at in heads]
    outs = []
    for h, at in enumerate(heads):
        top = jnp.max(scores[h], axis=0, keepdims=True)
        p = jnp.exp2((scores[h] - top) * scale)
        total = jnp.sum(p, axis=0, keepdims=True)
        outs.append((nn(values[at], p.astype(BF16)) * (1.0 / total)).astype(BF16))
        l_ref[h : h + 1, :] = top * scale + jnp.log2(total)
    o_ref[...] = jnp.concatenate(outs, axis=0).T


FORWARD_HEADS = 4
BACK_HEADS = 2


def attn(qkv, slot, prev, wait=()):
    slots, s, n = qkv.shape
    d = n // 3
    lanes = FORWARD_HEADS * HEAD_DIM
    groups = d // lanes

    def block(part):
        return spec((None, s, lanes), lambda j: (slot, 0, j + part * groups))

    return call(
        attn_kernel,
        "attn",
        (groups,),
        [(qkv, block(0)), (qkv, block(1)), (qkv, block(2))],
        [
            ((slots, s, d), BF16, block(0)),
            (
                (slots, groups, FORWARD_HEADS, s),
                F32,
                spec((None, None, FORWARD_HEADS, s), lambda j: (slot, j, 0, 0)),
            ),
        ],
        prev=prev,
        wait=wait,
        flops=4 * s * s * d * 3,
    )


def out_ln_kernel(c_ref, x_ref, w_ref, bo_ref, g_ref, b_ref, a_ref, n_ref):
    a = x_ref[...].astype(F32) + (nn(c_ref[...], w_ref[...]) + bo_ref[...].astype(F32))
    a_ref[...] = a
    u, _ = unit(a)
    n_ref[...] = (u * g_ref[...].astype(F32) + b_ref[...].astype(F32)).astype(BF16)


def out_ln(ctx, x, w, bias, gain, shift, slot, prev, wait=()):
    slots, s, d = ctx.shape
    at = fixed((None, s, d), (slot, 0, 0))
    vec = fixed((1, d))
    return call(
        out_ln_kernel,
        "out_ln",
        (1,),
        [
            (ctx, at),
            (x, fixed((s, d))),
            (w, fixed((d, d), (0, w.shape[1] // d - 1))),
            (bias, vec),
            (gain, vec),
            (shift, vec),
        ],
        [((slots, s, d), F32, at), ((slots, s, d), BF16, at)],
        prev=prev,
        wait=wait,
        flops=2 * s * d * d,
    )


def up_gelu_kernel(n_ref, w_ref, b_ref, h_ref, gp_ref):
    h, gp = gelu_parts(nn(n_ref[...], w_ref[...]) + b_ref[...].astype(F32))
    h_ref[...] = h.astype(BF16)
    gp_ref[...] = gp.astype(BF16)


def up_gelu(n2, w, bias, slot, prev, wait=()):
    slots, s, d = n2.shape
    n = w.shape[1]
    t = 512
    out = ((slots, s, n), BF16, spec((None, s, t), lambda j: (slot, 0, j)))
    return call(
        up_gelu_kernel,
        "up_gelu",
        (n // t,),
        [
            (n2, fixed((None, s, d), (slot, 0, 0))),
            (w, spec((d, t), lambda j: (0, j))),
            (bias, spec((1, t), lambda j: (0, j))),
        ],
        [out, out],
        prev=prev,
        wait=wait,
        flops=3 * s * d * n,
    )


def down_kernel(h_ref, w_ref, a_ref, b_ref, o_ref, acc):
    j = pl.program_id(0)

    @pl.when(j == 0)
    def _():
        acc[...] = a_ref[...] + b_ref[...].astype(F32)

    acc[...] += nn(h_ref[...], w_ref[...])

    @pl.when(j == pl.num_programs(0) - 1)
    def _():
        o_ref[...] = acc[...].astype(BF16)


def down(hidden, w, after, bias, slot, wait=()):
    _, s, n = hidden.shape
    d = w.shape[1]
    t = 1024
    return call(
        down_kernel,
        "down",
        (n // t,),
        [
            (hidden, spec((None, s, t), lambda j: (slot, 0, j))),
            (w, spec((t, d), lambda j: (j, 0))),
            (after, fixed((None, s, d), (slot, 0, 0))),
            (bias, fixed((1, d))),
        ],
        [((s, d), BF16, fixed((s, d)))],
        scratch=[pltpu.VMEM((s, d), F32)],
        wait=wait,
        flops=2 * s * d * n,
    )[0]


def mlp_back_kernel(
    at_ref, g_ref, gp_ref, wd_ref, wu_ref, a_ref, gain_ref, wo_ref,
    gu_ref, ga_ref, gt_ref, gc_ref, dbu_ref, sm_ref, acc,
):
    j = pl.program_id(0)
    gu = (nt(g_ref[...], wd_ref[...]) * gp_ref[...].astype(F32)).astype(BF16)
    gu_ref[...] = gu
    dbu_ref[...] = col_sum(gu)

    @pl.when(j == 0)
    def _():
        acc[...] = jnp.zeros_like(acc)

    acc[...] += nt(gu, wu_ref[...])

    @pl.when(j == pl.num_programs(0) - 1)
    def _():
        gn = acc[...]
        u, r = unit(a_ref[...])
        g = g_ref[...].astype(F32)
        ga = g + norm_back(gn, u, r, gain_ref[...].astype(F32))
        ga_ref[...] = ga
        gt = ga.astype(BF16)
        gt_ref[...] = gt
        gc_ref[...] = nt(gt, wo_ref[...]).astype(BF16)
        sm_ref[0:1, :] = col_sum(gn * u)
        sm_ref[1:2, :] = col_sum(gn)
        sm_ref[2:3, :] = col_sum(g)
        sm_ref[3:4, :] = col_sum(gt)


def mlp_back(at, g, gp, wd, wu, after, gain, wo, slot, slots, prev, wait=()):
    s, d = g.shape
    n = gp.shape[2]
    t = 512
    row = fixed((None, s, d), (slot, 0, 0))
    return call(
        mlp_back_kernel,
        "mlp_back",
        (n // t,),
        [
            (g, fixed((s, d))),
            (gp, spec((None, s, t), lambda j, r: (r[0], 0, j))),
            (wd, spec((t, d), lambda j, r: (j, 0))),
            (wu, spec((d, t), lambda j, r: (0, j))),
            (after, spec((None, s, d), lambda j, r: (r[0], 0, 0))),
            (gain, fixed((1, d))),
            (wo, fixed((d, d), (0, wo.shape[1] // d - 1))),
        ],
        [
            ((slots, s, n), BF16, spec((None, s, t), lambda j, r: (slot, 0, j))),
            ((s, d), F32, fixed((s, d))),
            ((slots, s, d), BF16, row),
            ((s, d), BF16, fixed((s, d))),
            ((slots, 1, n), F32, spec((None, 1, t), lambda j, r: (slot, 0, j))),
            ((slots, 4, d), F32, fixed((None, 4, d), (slot, 0, 0))),
        ],
        scratch=[pltpu.VMEM((s, d), F32)],
        scalars=at,
        prev=prev,
        wait=wait,
        flops=4 * s * d * n + 2 * s * d * d,
    )


def attn_back_kernel(at_ref, q_ref, k_ref, v_ref, do_ref, l_ref, o_ref):
    scale = LOG2E * HEAD_DIM**-0.5
    lanes = q_ref.shape[1]
    heads = head_slices(lanes // HEAD_DIM)
    j = pl.program_id(0)
    first_head = lax.rem(j, l_ref.shape[0] // len(heads)) * len(heads)
    kt, qt, dot = k_ref[...].T, q_ref[...].T, do_ref[...].T
    scores = [nt(k_ref[:, at], q_ref[:, at]) for at in heads]
    dps = [nt(v_ref[:, at], do_ref[:, at]) for at in heads]
    dqs, dks, dvs = [], [], []
    for h, at in enumerate(heads):
        p = jnp.exp2(scores[h] * scale - l_ref[pl.ds(first_head + h, 1), :])
        pdp = p * dps[h]
        ds = (pdp - p * jnp.sum(pdp, axis=0, keepdims=True)).astype(BF16)
        dvs.append(nt(dot[at], p.astype(BF16)).astype(BF16))
        dks.append((nt(qt[at], ds) * HEAD_DIM**-0.5).astype(BF16))
        dqs.append((nn(kt[at], ds) * HEAD_DIM**-0.5).astype(BF16))
    d = o_ref.shape[1] // 3
    for part, pieces in enumerate((dqs, dks, dvs)):
        first = pl.multiple_of(part * d + j * lanes, lanes)
        o_ref[:, pl.ds(first, lanes)] = jnp.concatenate(pieces, axis=0).T


def attn_back(at, qkv, gc, logs, slot, slots, prev, wait=()):
    _, s, n = qkv.shape
    d = n // 3
    lanes = BACK_HEADS * HEAD_DIM
    groups = d // lanes
    ratio = FORWARD_HEADS // BACK_HEADS

    def block(part):
        return spec((None, s, lanes), lambda j, r: (r[0], 0, j + part * groups))

    return call(
        attn_back_kernel,
        "attn_back",
        (groups,),
        [
            (qkv, block(0)),
            (qkv, block(1)),
            (qkv, block(2)),
            (gc, spec((s, lanes), lambda j, r: (0, j))),
            (
                logs,
                spec((None, None, FORWARD_HEADS, s), lambda j, r: (r[0], j // ratio, 0, 0)),
            ),
        ],
        [((slots, s, n), BF16, fixed((None, s, n), (slot, 0, 0)))],
        scalars=at,
        prev=prev,
        wait=wait,
        flops=10 * s * s * d * 3,
    )[0]


def qkv_back_kernel(at_ref, g_ref, w_ref, x_ref, ga_ref, gain_ref, o_ref, ob_ref, sm_ref):
    d = x_ref.shape[1]
    gn = nt(g_ref[...], w_ref[...])
    u, r = unit(x_ref[...].astype(F32))
    out = ga_ref[...] + norm_back(gn, u, r, gain_ref[...].astype(F32))
    o_ref[...] = out
    ob_ref[...] = out.astype(BF16)
    sm_ref[0:1, :] = col_sum(gn * u)
    sm_ref[1:2, :] = col_sum(gn)
    sm_ref[2:3, :] = col_sum(g_ref[:, 0:d])
    sm_ref[3:4, :] = col_sum(g_ref[:, 2 * d : 3 * d])


def qkv_back(at, gqkv, w, xb, ga, gain, slot, prev, wait=()):
    slots, s, n = gqkv.shape
    d = n // 3
    return call(
        qkv_back_kernel,
        "qkv_back",
        (1,),
        [
            (gqkv, fixed((None, s, n), (slot, 0, 0))),
            (w, fixed((d, n))),
            (xb, spec((None, s, d), lambda j, r: (r[0], 0, 0))),
            (ga, fixed((s, d))),
            (gain, fixed((1, d))),
        ],
        [
            ((s, d), F32, fixed((s, d))),
            ((s, d), BF16, fixed((s, d))),
            ((slots, 4, d), F32, fixed((None, 4, d), (slot, 0, 0))),
        ],
        scalars=at,
        prev=prev,
        wait=wait,
        flops=2 * s * d * n,
    )


def weight_grad_kernel(at_ref, a_ref, b0_ref, b1_ref, send_ref, keep_ref, left, right):
    s = b0_ref.shape[0]
    step = right.shape[0] // 2
    i = pl.program_id(0)

    @pl.when(i == 0)
    def _():
        right[...] = jnp.zeros_like(right)
        left[...] = jnp.zeros_like(left)
        for image in range(2):
            left[:, image * step : image * step + s] = a_ref[image].T

    right[0:s, :] = b0_ref[...]
    right[step : step + s, :] = b1_ref[...]
    owners, rows, cols = send_ref.shape
    out = nn(left[...], right[...]).astype(BF16).reshape(owners, rows, cols)

    @pl.when(i < pl.num_programs(0) // 2)
    def _():
        send_ref[...] = out

    @pl.when(i >= pl.num_programs(0) // 2)
    def _():
        keep_ref[...] = out


def weight_grad(at, left, right, owners, replicas, name, wait=()):
    _, s, m = left.shape
    n = right.shape[2]
    chips = replicas // CORES
    rows, cols = m // owners, n // replicas
    step = -(-s // 128) * 128

    def col(image):
        def index(i, r):
            core = jnp.where(i < chips, 1 - r[2], r[2])
            return (r[1] + image, 0, lax.rem(i, chips) * CORES + core)

        return spec((None, s, cols), index)

    def out(first):
        return (
            (chips, owners, rows, cols),
            BF16,
            spec(
                (None, owners, rows, cols),
                lambda i, r: (jnp.clip(i - first, 0, chips - 1), 0, 0, 0),
            ),
        )

    return call(
        weight_grad_kernel,
        name,
        (replicas,),
        [
            (left, spec((2, s, m), lambda i, r: (r[0], 0, 0))),
            (right, col(0)),
            (right, col(1)),
        ],
        [out(0), out(chips)],
        scratch=[pltpu.VMEM((m, 2 * step), BF16), pltpu.VMEM((2 * step, cols), BF16)],
        scalars=at,
        wait=wait,
        flops=4 * s * m * n,
    )


class Place:
    def __init__(self):
        self.owners = lax.axis_size("shard")
        self.replicas = lax.axis_size("rep")
        self.chips = self.replicas // CORES
        self.z = lax.axis_index("shard")
        rep = lax.axis_index("rep")
        self.rep = rep
        self.y = rep // CORES
        self.core = rep % CORES

    def ring_z(self, block, step=1):
        n = self.owners
        return lax.ppermute(block, "shard", [(i, (i + step) % n) for i in range(n)])

    def ring_y(self, block):
        n = self.chips
        route = [
            (y * CORES + c, ((y + 1) % n) * CORES + c) for y in range(n) for c in range(CORES)
        ]
        return lax.ppermute(block, "rep", route)

    def swap_core(self, block):
        route = [(i, i ^ 1) for i in range(self.replicas)]
        return lax.ppermute(block, "rep", route)


def gather_vector(place, vector):
    held = [vector] + [place.ring_z(vector, step) for step in range(1, place.owners)]
    order = lax.rem(place.z - jnp.arange(place.owners) + place.owners, place.owners)
    return jnp.take(jnp.stack(held), order, axis=0)


def zero_after(value):
    corner = lax.slice(value, (0,) * value.ndim, (1,) * value.ndim)
    return (corner.reshape(()).astype(F32) * 0.0).astype(jnp.int32)


def gather_whole(place, shards, *earlier):
    part = shards[0].shape[0] // place.replicas
    first = place.rep * part
    for value in earlier:
        first = first + zero_after(value)
    mine = [lax.dynamic_slice_in_dim(w, first, part, 0) for w in shards]
    return lax.all_gather(jnp.concatenate(mine, axis=1), ("shard", "rep"), axis=0, tiled=True)


def add(left, right):
    return (left.astype(F32) + right.astype(F32)).astype(BF16)


def pick(holder, index, axis):
    return lax.dynamic_index_in_dim(holder, index, axis, keepdims=False)


def finish_kernel(count, at_ref, *refs):
    pieces, out_ref = refs[:count], refs[-1]
    for i, piece in enumerate(pieces):
        cols = piece.shape[1]
        first = pl.multiple_of(at_ref[i] * cols, cols)
        out_ref[:, pl.ds(first, cols)] = piece[...].astype(F32)


def finish(pieces, parts, wait=()):
    rows, cols = pieces[0].shape
    whole = pl.BlockSpec(memory_space=pltpu.VMEM)
    out = pl.pallas_call(
        partial(finish_kernel, len(pieces)),
        in_specs=[pl.BlockSpec(memory_space=pltpu.SMEM)]
        + [whole] * len(pieces)
        + [pl.BlockSpec(memory_space=pl.ANY)] * len(wait),
        out_specs=whole,
        out_shape=jax.ShapeDtypeStruct((rows, cols * len(pieces)), F32),
        compiler_params=pltpu.CompilerParams(vmem_limit_bytes=VMEM_BYTES),
        cost_estimate=pl.CostEstimate(
            flops=0, bytes_accessed=0, transcendentals=0
        ),
        name="finish",
    )(jnp.stack(parts).astype(jnp.int32), *pieces, *wait)
    return out[None]


def reduce_chips(place, held):
    chips = place.chips
    total = pick(held, lax.rem(place.y + chips - 1, chips), 0)
    for step in range(1, chips):
        total = add(
            place.ring_y(total), pick(held, lax.rem(place.y + 2 * chips - 1 - step, chips), 0)
        )
    return total


def reduce_rows(place, held, *wait):
    total = lax.psum_scatter(held, "shard", scatter_dimension=0, tiled=True)[0]
    chips = place.chips
    pieces, parts = [], []
    for t in range(chips):
        if t > 0:
            total = place.ring_y(total)
        chip = lax.rem(place.y - t + chips, chips)
        pieces += [total, place.swap_core(total)]
        parts += [chip * CORES + place.core, chip * CORES + 1 - place.core]
    return finish(pieces, parts, wait)


def sum_small(place, table):
    total = table + place.swap_core(table)
    ring = total
    for _ in range(1, place.chips):
        ring = place.ring_y(ring)
        total = total + ring
    owners = place.owners
    out = pick(total, place.z, 0)
    for step in range(1, owners):
        out = out + place.ring_z(pick(total, lax.rem(place.z + step, owners), 0), step)
    return out[None]


def per_device(
    images, cotangent, ln1_scale, ln1_shift, w_qkv, bias_qv, w_out, bias_out,
    ln2_scale, ln2_shift, w_up, bias_up, w_down, bias_down,
):
    place = Place()
    section = lax.axis_index("section")
    first = section == 0
    _, s, d = images.shape

    vectors = (
        ln1_scale, ln1_shift, bias_qv, bias_out, ln2_scale, ln2_shift, bias_up, bias_down
    )
    widths = [v.shape[1] for v in vectors]
    packed = gather_vector(place, jnp.concatenate(vectors, axis=1)[0])
    wqo = gather_whole(place, (w_qkv[0], w_out[0]))
    wu = gather_whole(place, (w_up[0],))
    wd = gather_whole(place, (w_down[0],), wqo)

    whole = []
    start = 0
    for width in widths:
        whole.append(packed[:, start : start + width].reshape(1, -1))
        start += width
    gain1, shift1, bias_two, bias_o, gain2, shift2, bias_u, bias_d = whole
    bias_mixed = jnp.concatenate(
        [bias_two[:, :d], jnp.zeros((1, d), BF16), bias_two[:, d:]], axis=1
    )
    slots = 4
    xb = n1 = qkv = ctx = logs = after = n2 = hidden = gp = None

    def send_on(block):
        return lax.ppermute(block, "section", [(0, 1)])

    def send_back(block):
        return lax.ppermute(block, "section", [(1, 0)])

    def forward_attn(x, slot):
        nonlocal xb, n1, qkv, ctx, logs, after, n2
        xb, n1, qkv = ln_qkv(x, gain1, shift1, wqo, bias_mixed, slot, slots, (xb, n1, qkv))
        ctx, logs = attn(qkv, slot, (ctx, logs))
        after, n2 = out_ln(ctx, x, wqo, bias_o, gain2, shift2, slot, (after, n2))

    def forward_up(slot):
        nonlocal hidden, gp
        hidden, gp = up_gelu(n2, wu, bias_u, slot, (hidden, gp))

    def forward_down(slot, *earlier):
        return down(hidden, wd, after, bias_d, slot, earlier)

    gslots = 3
    gu = gt = gqkv = dbu = sm2 = sm1 = None

    def back_mlp(source, upstream, slot, *wait):
        nonlocal gu, gt, dbu, sm2
        gu, ga, gt, gc, dbu, sm2 = mlp_back(
            source, upstream, gp, wd, wu, after, gain2, wqo, slot, gslots,
            (gu, None, gt, None, dbu, sm2), wait,
        )
        return ga, gc

    def back_attn(source, gc, slot, *wait):
        nonlocal gqkv
        gqkv = attn_back(source, qkv, gc, logs, slot, gslots, (gqkv,), wait)

    def back_qkv(source, ga, slot, *wait):
        nonlocal sm1
        grad, low, sm1 = qkv_back(source, gqkv, wqo, xb, ga, gain1, slot, (None, None, sm1), wait)
        return grad, low

    def source_slot(value):
        return jnp.asarray(value, jnp.int32).reshape(1)

    xb, n1, qkv = ln_qkv(images[0], gain1, shift1, wqo, bias_mixed, 0, slots, (xb, n1, qkv))
    xb, n1, qkv = ln_qkv(images[1], gain1, shift1, wqo, bias_mixed, 1, slots, (xb, n1, qkv))
    ctx, logs = attn(qkv, 0, (ctx, logs))
    ctx, logs = attn(qkv, 1, (ctx, logs))
    after, n2 = out_ln(ctx, images[0], wqo, bias_o, gain2, shift2, 0, (after, n2))
    after, n2 = out_ln(ctx, images[1], wqo, bias_o, gain2, shift2, 1, (after, n2))
    hidden, gp = up_gelu(n2, wu, bias_u, 0, (hidden, gp))
    hidden, gp = up_gelu(n2, wu, bias_u, 1, (hidden, gp))
    out0 = forward_down(0)
    arrived0 = send_on(out0)
    out1 = forward_down(1, out0)
    arrived1 = send_on(out1)

    forward_attn(arrived0, 2)
    forward_up(2)
    source = source_slot(2)
    up0 = cotangent[0]
    ga, gc = back_mlp(source, up0, 0)
    back_attn(source, gc, 0)
    grad0, low0 = back_qkv(source, ga, 0)
    returned0 = send_back(low0)

    forward_attn(arrived1, 3)
    forward_up(3)
    source = source_slot(jnp.where(first, 0, 3))
    up1 = jnp.where(first, returned0, cotangent[1])
    ga, gc = back_mlp(source, up1, 1)
    back_attn(source, gc, 1)
    grad1, low1 = back_qkv(source, ga, 1)
    up2 = send_back(low1)

    out2 = forward_down(2, low1)
    out3 = forward_down(3, out2)
    section_out = jnp.where(first, jnp.stack([out0, out1]), jnp.stack([out2, out3]))
    at = jnp.stack([section, 1 - section, place.core]).astype(jnp.int32)

    sizes = (place.owners, place.replicas)

    def products(left, right, name, *earlier):
        sent, kept = weight_grad(at, left, right, *sizes, name, earlier)
        return add(kept, place.swap_core(sent))

    source = source_slot(1)
    h_down = products(hidden, jnp.stack([up0, up1, up2]), "dw_down", out2, out3)
    t_down = reduce_chips(place, h_down)
    ga, gc = back_mlp(source, up2, 2, h_down)
    h_up = products(n2, gu, "dw_up")
    t_up = reduce_chips(place, h_up)
    h_out = products(ctx, gt, "dw_out", t_down)
    t_out = reduce_chips(place, h_out)
    back_attn(source, gc, 2, h_out, h_up)
    h_qkv = products(n1, gqkv, "dw_qkv")
    t_qkv = reduce_chips(place, h_qkv)
    grad2, low2 = back_qkv(source, ga, 2, h_qkv, t_up)

    grad_in = jnp.where(
        first,
        jnp.stack([grad1, grad2]),
        jnp.stack([low0.astype(F32), low1.astype(F32)]),
    )
    gw_down = reduce_rows(place, t_down)
    gw_up = reduce_rows(place, t_up)
    gw_out = reduce_rows(place, t_out)
    gw_qkv = reduce_rows(place, t_qkv, gw_down, gw_up, gw_out, grad_in, section_out)

    def own(holder):
        pair = lax.dynamic_slice_in_dim(holder, 1 - section, 2, 0)
        return jnp.sum(pair, axis=0)

    sm1, sm2, dbu = own(sm1), own(sm2), own(dbu)
    smalls = (
        sm1[0:1], sm1[1:2], jnp.concatenate([sm1[2:3], sm1[3:4]], axis=1), sm2[3:4],
        sm2[0:1], sm2[1:2], dbu, sm2[2:3],
    )
    table = jnp.concatenate([v.reshape(place.owners, -1) for v in smalls], axis=1)
    mine = sum_small(place, table)
    shares = []
    start = 0
    for width in widths:
        shares.append(mine[:, start : start + width])
        start += width
    (g_ln1s, g_ln1b, g_bqv, g_bo, g_ln2s, g_ln2b, g_bu, g_bd) = shares
    return (
        section_out[None], grad_in[None], g_ln1s, g_ln1b, gw_qkv, g_bqv, gw_out, g_bo,
        g_ln2s, g_ln2b, gw_up, g_bu, gw_down, g_bd,
    )


def solution(mesh):
    batch = P(("shard", "rep"), None, None)
    layers = P("section", ("shard", "rep"), None, None)
    vec = P("section", "shard")
    mat = P("section", "shard", None)
    in_specs = (
        batch, batch, vec, vec, mat, vec, mat, vec, vec, vec, mat, vec, mat, vec
    )
    out_specs = (
        layers, layers, vec, vec, mat, vec, mat, vec, vec, vec, mat, vec, mat, vec
    )
    return jax.shard_map(
        per_device, mesh=mesh, in_specs=in_specs, out_specs=out_specs, check_vma=False
    )
```

```python
from functools import partial

import jax
import jax.numpy as jnp
from jax import lax
from jax.experimental import pallas as pl
from jax.experimental.pallas import tpu as pltpu
from jax.sharding import PartitionSpec as P

HEAD_DIM = 64
CORES = 2
NORM_EPSILON = 1e-06
LOG2E = 1.4426950408889634
VMEM_BYTES = 56 * 1024 * 1024
F32 = jnp.float32
BF16 = jnp.bfloat16
COST = 1


def nn(left, right):
    return jnp.dot(left, right, preferred_element_type=F32)


def nt(left, right):
    return lax.dot_general(left, right, (((1,), (1,)), ((), ())), preferred_element_type=F32)


def tn(left, right):
    return lax.dot_general(left, right, (((0,), (0,)), ((), ())), preferred_element_type=F32)


def unit(values):
    centred = values - jnp.mean(values, axis=-1, keepdims=True)
    inv = lax.rsqrt(jnp.mean(centred * centred, axis=-1, keepdims=True) + NORM_EPSILON)
    return centred * inv, inv


def norm_back(grad, unit_rows, inv, gain):
    e = grad * gain
    return inv * (
        e
        - jnp.mean(e, axis=-1, keepdims=True)
        - unit_rows * jnp.mean(e * unit_rows, axis=-1, keepdims=True)
    )


def col_sum(values):
    return jnp.sum(values.astype(F32), axis=0, keepdims=True)


def gelu_parts(x):
    cdf = 0.5 + 0.5 * lax.erf(x * 0.7071067811865476)
    return x * cdf, cdf + x * (jnp.exp2(x * x * (-0.5 * LOG2E)) * 0.3989422804014327)


def spec(shape, index):
    return pl.BlockSpec(shape, index)


def fixed(shape, at=None):
    at = (0,) * len(shape) if at is None else at
    return pl.BlockSpec(shape, lambda *_: at)


def call(kernel, name, grid, ins, outs, scratch=(), scalars=None, prev=None, wait=(), flops=0):
    arrays = [a for a, _ in ins]
    in_specs = [s for _, s in ins]
    body = kernel
    if len(wait) > 0:
        read, prev = len(ins) + (scalars is not None), prev or [None] * len(outs)
        arrays += list(wait)
        in_specs += [pl.BlockSpec(memory_space=pl.ANY)] * len(wait)
        ins = list(ins) + [(w, None) for w in wait]
        inner = kernel

        def kernel(*refs):
            inner(*refs[:read], *refs[read + len(wait) :])

        body = kernel
    aliases = {}
    n_scalar = 0 if scalars is None else 1
    if prev is not None:
        count = len(ins)
        held = [(i, p) for i, p in enumerate(prev) if p is not None]
        for k, (i, p) in enumerate(held):
            aliases[n_scalar + count + k] = i
            arrays.append(p)
            in_specs.append(pl.BlockSpec(memory_space=pl.ANY))

        def body(*refs):
            kernel(*refs[: n_scalar + count], *refs[n_scalar + count + len(held) :])

    cost = pl.CostEstimate(flops=int(flops * COST), bytes_accessed=0, transcendentals=0)
    params = pltpu.CompilerParams(
        dimension_semantics=("arbitrary",) * len(grid), vmem_limit_bytes=VMEM_BYTES
    )
    out_shape = [jax.ShapeDtypeStruct(s, d) for s, d, _ in outs]
    out_specs = [s for _, _, s in outs]
    if scalars is None:
        f = pl.pallas_call(
            body,
            grid=grid,
            in_specs=in_specs,
            out_specs=out_specs,
            out_shape=out_shape,
            scratch_shapes=list(scratch),
            input_output_aliases=aliases,
            compiler_params=params,
            cost_estimate=cost,
            name=name,
        )
        return f(*arrays)
    f = pl.pallas_call(
        body,
        grid_spec=pltpu.PrefetchScalarGridSpec(
            num_scalar_prefetch=1,
            grid=grid,
            in_specs=in_specs,
            out_specs=out_specs,
            scratch_shapes=list(scratch),
        ),
        out_shape=out_shape,
        input_output_aliases=aliases,
        compiler_params=params,
        cost_estimate=cost,
        name=name,
    )
    return f(scalars, *arrays)


def ln_qkv_kernel(x_ref, g_ref, b_ref, w_ref, bq_ref, xb_ref, n1_ref, o_ref):
    @pl.when(pl.program_id(0) == 0)
    def _():
        x = x_ref[...]
        xb_ref[...] = x
        u, _ = unit(x.astype(F32))
        n1_ref[...] = (u * g_ref[...].astype(F32) + b_ref[...].astype(F32)).astype(BF16)

    o_ref[...] = (nn(n1_ref[...], w_ref[...]) + bq_ref[...].astype(F32)).astype(BF16)


def ln_qkv(x, gain, shift, w, bias, slot, slots, prev, wait=()):
    s, d = x.shape
    n = bias.shape[1]
    t = 1024
    return call(
        ln_qkv_kernel,
        "ln_qkv",
        (n // t,),
        [
            (x, fixed((s, d))),
            (gain, fixed((1, d))),
            (shift, fixed((1, d))),
            (w, spec((d, t), lambda j: (0, j))),
            (bias, spec((1, t), lambda j: (0, j))),
        ],
        [
            ((slots, s, d), BF16, fixed((None, s, d), (slot, 0, 0))),
            ((slots, s, d), BF16, fixed((None, s, d), (slot, 0, 0))),
            ((slots, s, n), BF16, spec((None, s, t), lambda j: (slot, 0, j))),
        ],
        prev=prev,
        wait=wait,
        flops=2 * s * d * n,
    )


def head_slices(count):
    return [slice(h * HEAD_DIM, (h + 1) * HEAD_DIM) for h in range(count)]


def attn_kernel(q_ref, k_ref, v_ref, o_ref, l_ref):
    scale = LOG2E * HEAD_DIM**-0.5
    heads = head_slices(l_ref.shape[0])
    values = v_ref[...].T
    scores = [nt(k_ref[:, at], q_ref[:, at]) for at in heads]
    outs = []
    for h, at in enumerate(heads):
        top = jnp.max(scores[h], axis=0, keepdims=True)
        p = jnp.exp2((scores[h] - top) * scale)
        total = jnp.sum(p, axis=0, keepdims=True)
        outs.append((nn(values[at], p.astype(BF16)) * (1.0 / total)).astype(BF16))
        l_ref[h : h + 1, :] = top * scale + jnp.log2(total)
    o_ref[...] = jnp.concatenate(outs, axis=0).T


FORWARD_HEADS = 4
BACK_HEADS = 2


def attn(qkv, slot, prev, wait=()):
    slots, s, n = qkv.shape
    d = n // 3
    lanes = FORWARD_HEADS * HEAD_DIM
    groups = d // lanes

    def block(part):
        return spec((None, s, lanes), lambda j: (slot, 0, j + part * groups))

    return call(
        attn_kernel,
        "attn",
        (groups,),
        [(qkv, block(0)), (qkv, block(1)), (qkv, block(2))],
        [
            ((slots, s, d), BF16, block(0)),
            (
                (slots, groups, FORWARD_HEADS, s),
                F32,
                spec((None, None, FORWARD_HEADS, s), lambda j: (slot, j, 0, 0)),
            ),
        ],
        prev=prev,
        wait=wait,
        flops=4 * s * s * d * 3,
    )


def out_ln_kernel(c_ref, x_ref, w_ref, bo_ref, g_ref, b_ref, a_ref, n_ref):
    a = x_ref[...].astype(F32) + (nn(c_ref[...], w_ref[...]) + bo_ref[...].astype(F32))
    a_ref[...] = a
    u, _ = unit(a)
    n_ref[...] = (u * g_ref[...].astype(F32) + b_ref[...].astype(F32)).astype(BF16)


def out_ln(ctx, x, w, bias, gain, shift, slot, prev, wait=()):
    slots, s, d = ctx.shape
    at = fixed((None, s, d), (slot, 0, 0))
    vec = fixed((1, d))
    return call(
        out_ln_kernel,
        "out_ln",
        (1,),
        [
            (ctx, at),
            (x, fixed((s, d))),
            (w, fixed((d, d), (0, 3))),
            (bias, vec),
            (gain, vec),
            (shift, vec),
        ],
        [((slots, s, d), F32, at), ((slots, s, d), BF16, at)],
        prev=prev,
        wait=wait,
        flops=2 * s * d * d,
    )


def up_gelu_kernel(n_ref, w_ref, b_ref, h_ref, gp_ref):
    h, gp = gelu_parts(nn(n_ref[...], w_ref[...]) + b_ref[...].astype(F32))
    h_ref[...] = h.astype(BF16)
    gp_ref[...] = gp.astype(BF16)


def up_gelu(n2, w, bias, slot, prev):
    slots, s, d = n2.shape
    n = bias.shape[1]
    t = 512
    out = ((slots, s, n), BF16, spec((None, s, t), lambda j: (slot, 0, j)))
    return call(
        up_gelu_kernel,
        "up_gelu",
        (n // t,),
        [
            (n2, fixed((None, s, d), (slot, 0, 0))),
            (w, spec((d, t), lambda j: (0, 4 * d // t + j))),
            (bias, spec((1, t), lambda j: (0, j))),
        ],
        [out, out],
        prev=prev,
        flops=3 * s * d * n,
    )


def down_blocks(w, owners, count):
    d = w.shape[0]

    def block(k):
        return (w, spec((d // owners, d), lambda j, *_: (j, 8 + k)))

    return [block(k) for k in range(count)]


def down_kernel(h_ref, *refs):
    blocks, (a_ref, b_ref, o_ref, acc) = refs[:-4], refs[-4:]
    j = pl.program_id(0)
    rows = blocks[0].shape[0]
    part = sum(nn(h_ref[:, k * rows : (k + 1) * rows], b[...]) for k, b in enumerate(blocks))

    @pl.when(j == 0)
    def _():
        acc[...] = a_ref[...] + b_ref[...].astype(F32) + part

    @pl.when(j > 0)
    def _():
        acc[...] += part

    @pl.when(j == pl.num_programs(0) - 1)
    def _():
        o_ref[...] = acc[...].astype(BF16)


def down(hidden, w, after, bias, slot, owners, wait=()):
    _, s, n = hidden.shape
    d = w.shape[0]
    t = n // owners
    return call(
        down_kernel,
        "down",
        (owners,),
        [(hidden, spec((None, s, t), lambda j: (slot, 0, j)))]
        + down_blocks(w, owners, n // d)
        + [(after, fixed((None, s, d), (slot, 0, 0))), (bias, fixed((1, d)))],
        [((s, d), BF16, fixed((s, d)))],
        scratch=[pltpu.VMEM((s, d), F32)],
        wait=wait,
        flops=2 * s * d * n,
    )[0]


def mlp_back_kernel(at_ref, g_ref, gp_ref, wu_ref, gain_ref, a_hbm, wo_hbm, *refs):
    blocks, (gu_ref, ga_ref, gt_ref, gc_ref, dbu_ref, sm_ref, acc, a_ref, wo_ref, sems) = (
        refs[:-10],
        refs[-10:],
    )
    j = pl.program_id(0)
    d = a_ref.shape[1]
    copies = (
        pltpu.make_async_copy(a_hbm.at[at_ref[0]], a_ref, sems.at[0]),
        pltpu.make_async_copy(wo_hbm.at[:, pl.ds(3 * d, d)], wo_ref, sems.at[1]),
    )

    @pl.when(j == 0)
    def _():
        for copy in copies:
            copy.start()

    gh = jnp.concatenate([nt(g_ref[...], block[...]) for block in blocks], axis=1)
    gu = (gh * gp_ref[...].astype(F32)).astype(BF16)
    gu_ref[...] = gu
    dbu_ref[...] = col_sum(gu)
    part = nt(gu, wu_ref[...])

    @pl.when(j == 0)
    def _():
        acc[...] = part

    @pl.when(j > 0)
    def _():
        acc[...] += part

    @pl.when(j == pl.num_programs(0) - 1)
    def _():
        for copy in copies:
            copy.wait()
        gn = acc[...]
        u, r = unit(a_ref[...])
        g = g_ref[...].astype(F32)
        ga = g + norm_back(gn, u, r, gain_ref[...].astype(F32))
        ga_ref[...] = ga
        gt = ga.astype(BF16)
        gt_ref[...] = gt
        gc_ref[...] = nt(gt, wo_ref[...]).astype(BF16)
        sm_ref[0:1, :] = col_sum(gn * u)
        sm_ref[1:2, :] = col_sum(gn)
        sm_ref[2:3, :] = col_sum(g)
        sm_ref[3:4, :] = col_sum(gt)


def mlp_back(at, g, gp, w, after, gain, slot, slots, owners, prev, wait=()):
    s, d = g.shape
    n = gp.shape[2]
    t = n // owners
    row = fixed((None, s, d), (slot, 0, 0))
    anywhere = pl.BlockSpec(memory_space=pl.ANY)
    return call(
        mlp_back_kernel,
        "mlp_back",
        (owners,),
        [
            (g, fixed((s, d))),
            (gp, spec((None, s, t), lambda j, r: (r[0], 0, j))),
            (w, spec((d, t), lambda j, r: (0, 4 * d // t + j))),
            (gain, fixed((1, d))),
            (after, anywhere),
            (w, anywhere),
        ]
        + down_blocks(w, owners, n // d),
        [
            ((slots, s, n), BF16, spec((None, s, t), lambda j, r: (slot, 0, j))),
            ((s, d), F32, fixed((s, d))),
            ((slots, s, d), BF16, row),
            ((s, d), BF16, fixed((s, d))),
            ((slots, 1, n), F32, spec((None, 1, t), lambda j, r: (slot, 0, j))),
            ((slots, 4, d), F32, fixed((None, 4, d), (slot, 0, 0))),
        ],
        scratch=[
            pltpu.VMEM((s, d), F32),
            pltpu.VMEM((s, d), F32),
            pltpu.VMEM((d, d), BF16),
            pltpu.SemaphoreType.DMA((2,)),
        ],
        scalars=at,
        prev=prev,
        wait=wait,
        flops=4 * s * d * n + 2 * s * d * d,
    )


def attn_back_kernel(at_ref, q_ref, k_ref, v_ref, do_ref, l_ref, o_ref):
    scale = LOG2E * HEAD_DIM**-0.5
    lanes = q_ref.shape[1]
    heads = head_slices(lanes // HEAD_DIM)
    j = pl.program_id(0)
    first_head = lax.rem(j, l_ref.shape[0] // len(heads)) * len(heads)
    kt, qt, dot = k_ref[...].T, q_ref[...].T, do_ref[...].T
    scores = [nt(k_ref[:, at], q_ref[:, at]) for at in heads]
    dps = [nt(v_ref[:, at], do_ref[:, at]) for at in heads]
    dqs, dks, dvs = [], [], []
    for h, at in enumerate(heads):
        p = jnp.exp2(scores[h] * scale - l_ref[pl.ds(first_head + h, 1), :])
        pdp = p * dps[h]
        ds = (pdp - p * jnp.sum(pdp, axis=0, keepdims=True)).astype(BF16)
        dvs.append(nt(dot[at], p.astype(BF16)).astype(BF16))
        dks.append((nt(qt[at], ds) * HEAD_DIM**-0.5).astype(BF16))
        dqs.append((nn(kt[at], ds) * HEAD_DIM**-0.5).astype(BF16))
    d = o_ref.shape[1] // 3
    for part, pieces in enumerate((dqs, dks, dvs)):
        first = pl.multiple_of(part * d + j * lanes, lanes)
        o_ref[:, pl.ds(first, lanes)] = jnp.concatenate(pieces, axis=0).T


def attn_back(at, qkv, gc, logs, slot, slots, prev, wait=()):
    _, s, n = qkv.shape
    d = n // 3
    lanes = BACK_HEADS * HEAD_DIM
    groups = d // lanes
    ratio = FORWARD_HEADS // BACK_HEADS

    def block(part):
        return spec((None, s, lanes), lambda j, r: (r[0], 0, j + part * groups))

    return call(
        attn_back_kernel,
        "attn_back",
        (groups,),
        [
            (qkv, block(0)),
            (qkv, block(1)),
            (qkv, block(2)),
            (gc, spec((s, lanes), lambda j, r: (0, j))),
            (
                logs,
                spec((None, None, FORWARD_HEADS, s), lambda j, r: (r[0], j // ratio, 0, 0)),
            ),
        ],
        [((slots, s, n), BF16, fixed((None, s, n), (slot, 0, 0)))],
        scalars=at,
        prev=prev,
        wait=wait,
        flops=10 * s * s * d * 3,
    )[0]


def qkv_back_kernel(at_ref, g_ref, w_ref, x_ref, ga_ref, gain_ref, o_ref, ob_ref, sm_ref):
    d = x_ref.shape[1]
    gn = nt(g_ref[...], w_ref[...])
    u, r = unit(x_ref[...].astype(F32))
    out = ga_ref[...] + norm_back(gn, u, r, gain_ref[...].astype(F32))
    o_ref[...] = out
    ob_ref[...] = out.astype(BF16)
    sm_ref[0:1, :] = col_sum(gn * u)
    sm_ref[1:2, :] = col_sum(gn)
    sm_ref[2:3, :] = col_sum(g_ref[:, 0:d])
    sm_ref[3:4, :] = col_sum(g_ref[:, 2 * d : 3 * d])


def qkv_back(at, gqkv, w, xb, ga, gain, slot, prev, wait=()):
    slots, s, n = gqkv.shape
    d = n // 3
    return call(
        qkv_back_kernel,
        "qkv_back",
        (1,),
        [
            (gqkv, fixed((None, s, n), (slot, 0, 0))),
            (w, fixed((d, n))),
            (xb, spec((None, s, d), lambda j, r: (r[0], 0, 0))),
            (ga, fixed((s, d))),
            (gain, fixed((1, d))),
        ],
        [
            ((s, d), F32, fixed((s, d))),
            ((s, d), BF16, fixed((s, d))),
            ((slots, 4, d), F32, fixed((None, 4, d), (slot, 0, 0))),
        ],
        scalars=at,
        prev=prev,
        wait=wait,
        flops=2 * s * d * n,
    )


def weight_grad_kernel(at_ref, a_ref, b0_ref, b1_ref, send_ref, keep_ref, left, right):
    s = b0_ref.shape[0]
    step = right.shape[0] // 2
    i = pl.program_id(0)

    @pl.when(i == 0)
    def _():
        right[...] = jnp.zeros_like(right)
        left[...] = jnp.zeros_like(left)
        for image in range(2):
            left[:, image * step : image * step + s] = a_ref[image].T

    right[0:s, :] = b0_ref[...]
    right[step : step + s, :] = b1_ref[...]
    owners, rows, cols = send_ref.shape
    out = nn(left[...], right[...]).astype(BF16).reshape(owners, rows, cols)

    @pl.when(i < pl.num_programs(0) // 2)
    def _():
        send_ref[...] = out

    @pl.when(i >= pl.num_programs(0) // 2)
    def _():
        keep_ref[...] = out


def weight_grad(at, left, right, owners, replicas, name, wait=()):
    _, s, m = left.shape
    n = right.shape[2]
    chips = replicas // CORES
    rows, cols = m // owners, n // replicas
    step = -(-s // 128) * 128

    def col(image):
        def index(i, r):
            core = jnp.where(i < chips, 1 - r[2], r[2])
            return (r[1] + image, 0, lax.rem(i, chips) * CORES + core)

        return spec((None, s, cols), index)

    def out(first):
        return (
            (chips, owners, rows, cols),
            BF16,
            spec(
                (None, owners, rows, cols),
                lambda i, r: (jnp.clip(i - first, 0, chips - 1), 0, 0, 0),
            ),
        )

    return call(
        weight_grad_kernel,
        name,
        (replicas,),
        [
            (left, spec((2, s, m), lambda i, r: (r[0], 0, 0))),
            (right, col(0)),
            (right, col(1)),
        ],
        [out(0), out(chips)],
        scratch=[pltpu.VMEM((m, 2 * step), BF16), pltpu.VMEM((2 * step, cols), BF16)],
        scalars=at,
        wait=wait,
        flops=4 * s * m * n,
    )


class Place:
    def __init__(self):
        self.owners = lax.axis_size("shard")
        self.replicas = lax.axis_size("rep")
        self.chips = self.replicas // CORES
        self.z = lax.axis_index("shard")
        rep = lax.axis_index("rep")
        self.rep = rep
        self.y = rep // CORES
        self.core = rep % CORES

    def ring_z(self, block, step=1):
        n = self.owners
        return lax.ppermute(block, "shard", [(i, (i + step) % n) for i in range(n)])

    def ring_y(self, block):
        n = self.chips
        route = [
            (y * CORES + c, ((y + 1) % n) * CORES + c) for y in range(n) for c in range(CORES)
        ]
        return lax.ppermute(block, "rep", route)

    def swap_core(self, block):
        route = [(i, i ^ 1) for i in range(self.replicas)]
        return lax.ppermute(block, "rep", route)


def gather_vector(place, vector):
    held = [vector] + [place.ring_z(vector, step) for step in range(1, place.owners)]
    order = lax.rem(place.z - jnp.arange(place.owners) + place.owners, place.owners)
    return jnp.take(jnp.stack(held), order, axis=0)


def zero_after(value):
    corner = lax.slice(value, (0,) * value.ndim, (1,) * value.ndim)
    return (corner.reshape(()).astype(F32) * 0.0).astype(jnp.int32)


def gather_weights(place, w_qkv, w_out, w_up, w_down):
    rows, d = w_out.shape
    part = rows // place.replicas
    first = place.rep * part
    blocks = [w_down[k : k + rows] for k in range(0, w_down.shape[0], rows)]
    whole = jnp.concatenate([w_qkv, w_out, w_up] + blocks, axis=1)
    mine = lax.dynamic_slice_in_dim(whole, first, part, 0)
    return lax.all_gather(mine, ("shard", "rep"), axis=0, tiled=True)


def add(left, right):
    return (left.astype(F32) + right.astype(F32)).astype(BF16)


def pick(holder, index, axis):
    return lax.dynamic_index_in_dim(holder, index, axis, keepdims=False)


def finish_kernel(count, at_ref, *refs):
    pieces, out_ref = refs[:count], refs[-1]
    for i, piece in enumerate(pieces):
        cols = piece.shape[1]
        first = pl.multiple_of(at_ref[i] * cols, cols)
        out_ref[:, pl.ds(first, cols)] = piece[...].astype(F32)


def finish(pieces, parts, wait=()):
    rows, cols = pieces[0].shape
    whole = pl.BlockSpec(memory_space=pltpu.VMEM)
    out = pl.pallas_call(
        partial(finish_kernel, len(pieces)),
        in_specs=[pl.BlockSpec(memory_space=pltpu.SMEM)]
        + [whole] * len(pieces)
        + [pl.BlockSpec(memory_space=pl.ANY)] * len(wait),
        out_specs=whole,
        out_shape=jax.ShapeDtypeStruct((rows, cols * len(pieces)), F32),
        compiler_params=pltpu.CompilerParams(vmem_limit_bytes=VMEM_BYTES),
        cost_estimate=pl.CostEstimate(
            flops=0, bytes_accessed=0, transcendentals=0
        ),
        name="finish",
    )(jnp.stack(parts).astype(jnp.int32), *pieces, *wait)
    return out[None]


def reduce_chips(place, held):
    chips = place.chips
    total = pick(held, lax.rem(place.y + chips - 1, chips), 0)
    for step in range(1, chips):
        total = add(
            place.ring_y(total), pick(held, lax.rem(place.y + 2 * chips - 1 - step, chips), 0)
        )
    return total


def reduce_rows(place, held, *wait):
    total = lax.psum_scatter(held, "shard", scatter_dimension=0, tiled=True)[0]
    chips = place.chips
    pieces, parts = [], []
    for t in range(chips):
        if t > 0:
            total = place.ring_y(total)
        chip = lax.rem(place.y - t + chips, chips)
        pieces += [total, place.swap_core(total)]
        parts += [chip * CORES + place.core, chip * CORES + 1 - place.core]
    return finish(pieces, parts, wait)


def sum_small(place, table):
    total = table + place.swap_core(table)
    ring = total
    for _ in range(1, place.chips):
        ring = place.ring_y(ring)
        total = total + ring
    owners = place.owners
    out = pick(total, place.z, 0)
    for step in range(1, owners):
        out = out + place.ring_z(pick(total, lax.rem(place.z + step, owners), 0), step)
    return out[None]


def per_device(
    images, cotangent, ln1_scale, ln1_shift, w_qkv, bias_qv, w_out, bias_out,
    ln2_scale, ln2_shift, w_up, bias_up, w_down, bias_down,
):
    place = Place()
    section = lax.axis_index("section")
    first = section == 0
    _, s, d = images.shape

    vectors = (
        ln1_scale, ln1_shift, bias_qv, bias_out, ln2_scale, ln2_shift, bias_up, bias_down
    )
    widths = [v.shape[1] for v in vectors]
    packed = gather_vector(place, jnp.concatenate(vectors, axis=1)[0])
    w = gather_weights(place, w_qkv[0], w_out[0], w_up[0], w_down[0])

    whole = []
    start = 0
    for width in widths:
        whole.append(packed[:, start : start + width].reshape(1, -1))
        start += width
    gain1, shift1, bias_two, bias_o, gain2, shift2, bias_u, bias_d = whole
    bias_mixed = jnp.concatenate(
        [bias_two[:, :d], jnp.zeros((1, d), BF16), bias_two[:, d:]], axis=1
    )
    slots = 4
    xb = n1 = qkv = ctx = logs = after = n2 = hidden = gp = None

    def send_on(block):
        return lax.ppermute(block, "section", [(0, 1)])

    def send_back(block):
        return lax.ppermute(block, "section", [(1, 0)])

    def forward_attn(x, slot, *wait):
        nonlocal xb, n1, qkv, ctx, logs, after, n2
        prev = (xb, n1, qkv)
        xb, n1, qkv = ln_qkv(x, gain1, shift1, w, bias_mixed, slot, slots, prev, wait)
        ctx, logs = attn(qkv, slot, (ctx, logs))
        after, n2 = out_ln(ctx, x, w, bias_o, gain2, shift2, slot, (after, n2))

    def forward_up(slot):
        nonlocal hidden, gp
        hidden, gp = up_gelu(n2, w, bias_u, slot, (hidden, gp))

    def forward_down(slot, *earlier):
        return down(hidden, w, after, bias_d, slot, place.owners, earlier)

    gslots = 3
    gu = gt = gqkv = dbu = sm2 = sm1 = None

    def back_mlp(source, upstream, slot, *wait):
        nonlocal gu, gt, dbu, sm2
        gu, ga, gt, gc, dbu, sm2 = mlp_back(
            source, upstream, gp, w, after, gain2, slot, gslots, place.owners,
            (gu, None, gt, None, dbu, sm2), wait,
        )
        return ga, gc

    def back_attn(source, gc, slot, *wait):
        nonlocal gqkv
        gqkv = attn_back(source, qkv, gc, logs, slot, gslots, (gqkv,), wait)

    def back_qkv(source, ga, slot, *wait):
        nonlocal sm1
        grad, low, sm1 = qkv_back(source, gqkv, w, xb, ga, gain1, slot, (None, None, sm1), wait)
        return grad, low

    def source_slot(value):
        return jnp.asarray(value, jnp.int32).reshape(1)

    forward_attn(images[0], 0)
    forward_up(0)
    out0 = forward_down(0)
    arrived0 = send_on(out0)
    forward_attn(images[1], 1, out0)
    forward_up(1)
    out1 = forward_down(1)
    arrived1 = send_on(out1)

    forward_attn(arrived0, 2)
    forward_up(2)
    source = source_slot(2)
    up0 = cotangent[0]
    ga, gc = back_mlp(source, up0, 0)
    back_attn(source, gc, 0)
    grad0, low0 = back_qkv(source, ga, 0)
    returned0 = send_back(low0)

    forward_attn(arrived1, 3)
    forward_up(3)
    source = source_slot(jnp.where(first, 0, 3))
    up1 = jnp.where(first, returned0, cotangent[1])
    ga, gc = back_mlp(source, up1, 1)
    back_attn(source, gc, 1)
    grad1, low1 = back_qkv(source, ga, 1)
    up2 = send_back(low1)

    out2 = forward_down(2, low1)
    out3 = forward_down(3, out2)
    section_out = jnp.where(first, jnp.stack([out0, out1]), jnp.stack([out2, out3]))
    at = jnp.stack([section, 1 - section, place.core]).astype(jnp.int32)

    sizes = (place.owners, place.replicas)

    def products(left, right, name, *earlier):
        sent, kept = weight_grad(at, left, right, *sizes, name, earlier)
        return add(kept, place.swap_core(sent))

    source = source_slot(1)
    h_down = products(hidden, jnp.stack([up0, up1, up2]), "dw_down", out2, out3)
    t_down = reduce_chips(place, h_down)
    ga, gc = back_mlp(source, up2, 2, h_down)
    h_up = products(n2, gu, "dw_up")
    t_up = reduce_chips(place, h_up)
    h_out = products(ctx, gt, "dw_out", t_down)
    t_out = reduce_chips(place, h_out)
    back_attn(source, gc, 2, h_out, h_up)
    h_qkv = products(n1, gqkv, "dw_qkv")
    t_qkv = reduce_chips(place, h_qkv)
    grad2, low2 = back_qkv(source, ga, 2, h_qkv, t_up)

    grad_in = jnp.where(
        first,
        jnp.stack([grad1, grad2]),
        jnp.stack([low0.astype(F32), low1.astype(F32)]),
    )
    gw_down = reduce_rows(place, t_down)
    gw_up = reduce_rows(place, t_up)
    gw_out = reduce_rows(place, t_out)
    gw_qkv = reduce_rows(place, t_qkv, gw_down, gw_up, gw_out, grad_in, section_out)

    def own(holder):
        pair = lax.dynamic_slice_in_dim(holder, 1 - section, 2, 0)
        return jnp.sum(pair, axis=0)

    sm1, sm2, dbu = own(sm1), own(sm2), own(dbu)
    smalls = (
        sm1[0:1], sm1[1:2], jnp.concatenate([sm1[2:3], sm1[3:4]], axis=1), sm2[3:4],
        sm2[0:1], sm2[1:2], dbu, sm2[2:3],
    )
    table = jnp.concatenate([v.reshape(place.owners, -1) for v in smalls], axis=1)
    mine = sum_small(place, table)
    shares = []
    start = 0
    for width in widths:
        shares.append(mine[:, start : start + width])
        start += width
    (g_ln1s, g_ln1b, g_bqv, g_bo, g_ln2s, g_ln2b, g_bu, g_bd) = shares
    return (
        section_out[None], grad_in[None], g_ln1s, g_ln1b, gw_qkv, g_bqv, gw_out, g_bo,
        g_ln2s, g_ln2b, gw_up, g_bu, gw_down, g_bd,
    )


def solution(mesh):
    batch = P(("shard", "rep"), None, None)
    layers = P("section", ("shard", "rep"), None, None)
    vec = P("section", "shard")
    mat = P("section", "shard", None)
    in_specs = (
        batch, batch, vec, vec, mat, vec, mat, vec, vec, vec, mat, vec, mat, vec
    )
    out_specs = (
        layers, layers, vec, vec, mat, vec, mat, vec, vec, vec, mat, vec, mat, vec
    )
    return jax.shard_map(
        per_device, mesh=mesh, in_specs=in_specs, out_specs=out_specs, check_vma=False
    )
```

```python
from functools import partial

import jax
import jax.numpy as jnp
from jax import lax
from jax.experimental import pallas as pl
from jax.experimental.pallas import tpu as pltpu
from jax.sharding import PartitionSpec as P

HEAD_DIM = 64
CORES = 2
NORM_EPSILON = 1e-06
LOG2E = 1.4426950408889634
VMEM_BYTES = 56 * 1024 * 1024
F32 = jnp.float32
BF16 = jnp.bfloat16
COST = 1


def nn(left, right):
    return jnp.dot(left, right, preferred_element_type=F32)


def nt(left, right):
    return lax.dot_general(left, right, (((1,), (1,)), ((), ())), preferred_element_type=F32)


def tn(left, right):
    return lax.dot_general(left, right, (((0,), (0,)), ((), ())), preferred_element_type=F32)


def unit(values):
    centred = values - jnp.mean(values, axis=-1, keepdims=True)
    inv = lax.rsqrt(jnp.mean(centred * centred, axis=-1, keepdims=True) + NORM_EPSILON)
    return centred * inv, inv


def norm_back(grad, unit_rows, inv, gain):
    e = grad * gain
    return inv * (
        e
        - jnp.mean(e, axis=-1, keepdims=True)
        - unit_rows * jnp.mean(e * unit_rows, axis=-1, keepdims=True)
    )


def col_sum(values):
    return jnp.sum(values.astype(F32), axis=0, keepdims=True)


def gelu_parts(x):
    cdf = 0.5 + 0.5 * lax.erf(x * 0.7071067811865476)
    return x * cdf, cdf + x * (jnp.exp2(x * x * (-0.5 * LOG2E)) * 0.3989422804014327)


def spec(shape, index):
    return pl.BlockSpec(shape, index)


def fixed(shape, at=None):
    at = (0,) * len(shape) if at is None else at
    return pl.BlockSpec(shape, lambda *_: at)


def call(kernel, name, grid, ins, outs, scratch=(), scalars=None, prev=None, wait=(), flops=0):
    arrays = [a for a, _ in ins]
    in_specs = [s for _, s in ins]
    body = kernel
    if len(wait) > 0:
        read, prev = len(ins) + (scalars is not None), prev or [None] * len(outs)
        arrays += list(wait)
        in_specs += [pl.BlockSpec(memory_space=pl.ANY)] * len(wait)
        ins = list(ins) + [(w, None) for w in wait]
        inner = kernel

        def kernel(*refs):
            inner(*refs[:read], *refs[read + len(wait) :])

        body = kernel
    aliases = {}
    n_scalar = 0 if scalars is None else 1
    if prev is not None:
        count = len(ins)
        held = [(i, p) for i, p in enumerate(prev) if p is not None]
        for k, (i, p) in enumerate(held):
            aliases[n_scalar + count + k] = i
            arrays.append(p)
            in_specs.append(pl.BlockSpec(memory_space=pl.ANY))

        def body(*refs):
            kernel(*refs[: n_scalar + count], *refs[n_scalar + count + len(held) :])

    cost = pl.CostEstimate(flops=int(flops * COST), bytes_accessed=0, transcendentals=0)
    params = pltpu.CompilerParams(
        dimension_semantics=("arbitrary",) * len(grid), vmem_limit_bytes=VMEM_BYTES
    )
    out_shape = [jax.ShapeDtypeStruct(s, d) for s, d, _ in outs]
    out_specs = [s for _, _, s in outs]
    if scalars is None:
        f = pl.pallas_call(
            body,
            grid=grid,
            in_specs=in_specs,
            out_specs=out_specs,
            out_shape=out_shape,
            scratch_shapes=list(scratch),
            input_output_aliases=aliases,
            compiler_params=params,
            cost_estimate=cost,
            name=name,
        )
        return f(*arrays)
    f = pl.pallas_call(
        body,
        grid_spec=pltpu.PrefetchScalarGridSpec(
            num_scalar_prefetch=1,
            grid=grid,
            in_specs=in_specs,
            out_specs=out_specs,
            scratch_shapes=list(scratch),
        ),
        out_shape=out_shape,
        input_output_aliases=aliases,
        compiler_params=params,
        cost_estimate=cost,
        name=name,
    )
    return f(scalars, *arrays)


def head_slices(count):
    return [slice(h * HEAD_DIM, (h + 1) * HEAD_DIM) for h in range(count)]


def attend(q, k, v):
    scale = LOG2E * HEAD_DIM**-0.5
    heads = head_slices(q.shape[1] // HEAD_DIM)
    values = v.T
    scores = [nt(k[:, at], q[:, at]) for at in heads]
    outs, logs = [], []
    for h, at in enumerate(heads):
        top = jnp.max(scores[h], axis=0, keepdims=True)
        p = jnp.exp2((scores[h] - top) * scale)
        total = jnp.sum(p, axis=0, keepdims=True)
        outs.append((nn(values[at], p.astype(BF16)) * (1.0 / total)).astype(BF16))
        logs.append(top * scale + jnp.log2(total))
    return jnp.concatenate(outs, axis=0).T, logs


FORWARD_HEADS = 4
BACK_HEADS = 2


def down_blocks(w, owners, count):
    d = w.shape[0]

    def block(k):
        return (w, spec((d // owners, d), lambda j, *_: (j, 8 + k)))

    return [block(k) for k in range(count)]


def down_kernel(h_ref, *refs):
    blocks, (a_ref, b_ref, o_ref, acc) = refs[:-4], refs[-4:]
    j = pl.program_id(0)
    rows = blocks[0].shape[0]
    part = sum(nn(h_ref[:, k * rows : (k + 1) * rows], b[...]) for k, b in enumerate(blocks))

    @pl.when(j == 0)
    def _():
        acc[...] = a_ref[...] + b_ref[...].astype(F32) + part

    @pl.when(j > 0)
    def _():
        acc[...] += part

    @pl.when(j == pl.num_programs(0) - 1)
    def _():
        o_ref[...] = acc[...].astype(BF16)


def down(hidden, w, after, bias, slot, owners, wait=()):
    _, s, n = hidden.shape
    d = w.shape[0]
    t = n // owners
    return call(
        down_kernel,
        "down",
        (owners,),
        [(hidden, spec((None, s, t), lambda j: (slot, 0, j)))]
        + down_blocks(w, owners, n // d)
        + [(after, fixed((None, s, d), (slot, 0, 0))), (bias, fixed((1, d)))],
        [((s, d), BF16, fixed((s, d)))],
        scratch=[pltpu.VMEM((s, d), F32)],
        wait=wait,
        flops=2 * s * d * n,
    )[0]


UP_TILE = 512


def front_kernel(slot, count, *refs):
    (x_ref, g1_ref, s1_ref, w_ref, bq_ref, bo_ref, g2_ref, s2_ref, wu_ref, bu_ref) = refs[:10]
    blocks = refs[10 : 10 + count]
    rest = refs[10 + count :]
    if count > 0:
        bd_ref, rest = rest[0], rest[1:]
    outs, (h_ref, gp_ref), rest = rest[:7], rest[7:9], rest[9:]
    if count > 0:
        out_ref, rest = rest[0], rest[1:]
    n1_ref, qkv_ref, ctx_ref, logs_ref, a_ref, n2_ref, sems = rest[:7]
    j = pl.program_id(0)
    d = x_ref.shape[1]
    groups = logs_ref.shape[0]
    lanes = d // groups
    out_step = 3 + groups
    ups = 4 * d // UP_TILE
    copies = [
        pltpu.make_async_copy(ref, out.at[slot], sems.at[i])
        for i, (ref, out) in enumerate(
            zip((x_ref, n1_ref, qkv_ref, ctx_ref, logs_ref, a_ref, n2_ref), outs)
        )
    ]

    @pl.when(j == 0)
    def _():
        u, _ = unit(x_ref[...].astype(F32))
        n1_ref[...] = (u * g1_ref[...].astype(F32) + s1_ref[...].astype(F32)).astype(BF16)
        copies[0].start()
        copies[1].start()

    @pl.when(j < 3)
    def _():
        first = pl.multiple_of(j * d, d)
        qkv_ref[:, pl.ds(first, d)] = (
            nn(n1_ref[...], w_ref[...]) + bq_ref[...].astype(F32)
        ).astype(BF16)

    @pl.when(j == 2)
    def _():
        copies[2].start()

    @pl.when((j >= 3) & (j < out_step))
    def _():
        group = j - 3
        q, k, v = [
            qkv_ref[:, pl.ds(pl.multiple_of(part * d + group * lanes, lanes), lanes)]
            for part in range(3)
        ]
        ctx, logs = attend(q, k, v)
        ctx_ref[:, pl.ds(pl.multiple_of(group * lanes, lanes), lanes)] = ctx
        for h, log in enumerate(logs):
            logs_ref[group, h : h + 1, :] = log

    @pl.when(j == out_step)
    def _():
        copies[3].start()
        copies[4].start()
        a = x_ref[...].astype(F32) + (nn(ctx_ref[...], w_ref[...]) + bo_ref[...].astype(F32))
        a_ref[...] = a
        u, _ = unit(a)
        n2_ref[...] = (u * g2_ref[...].astype(F32) + s2_ref[...].astype(F32)).astype(BF16)
        copies[5].start()
        copies[6].start()

    @pl.when((j > out_step) & (j <= out_step + ups))
    def _():
        h, gp = gelu_parts(nn(n2_ref[...], wu_ref[...]) + bu_ref[...].astype(F32))
        h = h.astype(BF16)
        h_ref[...] = h
        gp_ref[...] = gp.astype(BF16)
        if count > 0:
            first = pl.multiple_of((j - out_step - 1) * UP_TILE, UP_TILE)
            rest[7][:, pl.ds(first, UP_TILE)] = h

    if count > 0:
        hidden, acc = rest[7], rest[8]

        @pl.when(j > out_step + ups)
        def _():
            owner = j - out_step - ups - 1
            rows = blocks[0].shape[0]
            part = sum(
                nn(
                    hidden[:, pl.ds(pl.multiple_of((owner * count + k) * rows, rows), rows)],
                    block[...],
                )
                for k, block in enumerate(blocks)
            )

            @pl.when(owner == 0)
            def _():
                acc[...] = a_ref[...] + bd_ref[...].astype(F32) + part

            @pl.when(owner > 0)
            def _():
                acc[...] += part

            @pl.when(j == pl.num_programs(0) - 1)
            def _():
                out_ref[...] = acc[...].astype(BF16)

    @pl.when(j == pl.num_programs(0) - 1)
    def _():
        for copy in copies:
            copy.wait()


def front(x, w, vectors, slot, slots, owners, prev, with_down):
    gain1, shift1, bias_q, bias_o, gain2, shift2, bias_u, bias_d = vectors
    s, d = x.shape
    n = bias_u.shape[1]
    groups = d // (FORWARD_HEADS * HEAD_DIM)
    first_up = 4 + groups
    ups = n // UP_TILE
    count = n // d if with_down else 0
    steps = first_up + ups + (owners if with_down else 0)

    def up_at(j):
        return jnp.clip(j - first_up, 0, ups - 1)

    def down_block(k):
        return (
            w,
            spec((d // owners, d), lambda j: (jnp.clip(j - first_up - ups, 0, owners - 1), 8 + k)),
        )

    vec = fixed((1, d))
    ins = [
        (x, fixed((s, d))),
        (gain1, vec),
        (shift1, vec),
        (w, spec((d, d), lambda j: (0, jnp.minimum(j, 3)))),
        (bias_q, spec((1, d), lambda j: (0, jnp.minimum(j, 2)))),
        (bias_o, vec),
        (gain2, vec),
        (shift2, vec),
        (w, spec((d, UP_TILE), lambda j: (0, 4 * d // UP_TILE + up_at(j)))),
        (bias_u, spec((1, UP_TILE), lambda j: (0, up_at(j)))),
    ] + [down_block(k) for k in range(count)]
    anywhere = pl.BlockSpec(memory_space=pl.ANY)
    tile = spec((None, s, UP_TILE), lambda j: (slot, 0, up_at(j)))
    outs = [
        ((slots, s, d), BF16, anywhere),
        ((slots, s, d), BF16, anywhere),
        ((slots, s, 3 * d), BF16, anywhere),
        ((slots, s, d), BF16, anywhere),
        ((slots, groups, FORWARD_HEADS, s), F32, anywhere),
        ((slots, s, d), F32, anywhere),
        ((slots, s, d), BF16, anywhere),
        ((slots, s, n), BF16, tile),
        ((slots, s, n), BF16, tile),
    ]
    scratch = [
        pltpu.VMEM((s, d), BF16),
        pltpu.VMEM((s, 3 * d), BF16),
        pltpu.VMEM((s, d), BF16),
        pltpu.VMEM((groups, FORWARD_HEADS, s), F32),
        pltpu.VMEM((s, d), F32),
        pltpu.VMEM((s, d), BF16),
        pltpu.SemaphoreType.DMA((7,)),
    ]
    prev = list(prev)
    if with_down:
        ins.append((bias_d, vec))
        outs.append(((s, d), BF16, fixed((s, d))))
        scratch += [pltpu.VMEM((s, n), BF16), pltpu.VMEM((s, d), F32)]
        prev.append(None)
    return call(
        partial(front_kernel, slot, count),
        "front",
        (steps,),
        ins,
        outs,
        scratch=scratch,
        prev=prev,
        flops=8 * s * d * d + 12 * s * s * d + 3 * s * d * n + (2 * s * d * n if with_down else 0),
    )


def mlp_back_kernel(at_ref, g_ref, gp_ref, wu_ref, gain_ref, a_hbm, wo_hbm, *refs):
    blocks, (gu_ref, ga_ref, gt_ref, gc_ref, dbu_ref, sm_ref, acc, a_ref, wo_ref, sems) = (
        refs[:-10],
        refs[-10:],
    )
    j = pl.program_id(0)
    d = a_ref.shape[1]
    copies = (
        pltpu.make_async_copy(a_hbm.at[at_ref[0]], a_ref, sems.at[0]),
        pltpu.make_async_copy(wo_hbm.at[:, pl.ds(3 * d, d)], wo_ref, sems.at[1]),
    )

    @pl.when(j == 0)
    def _():
        for copy in copies:
            copy.start()

    gh = jnp.concatenate([nt(g_ref[...], block[...]) for block in blocks], axis=1)
    gu = (gh * gp_ref[...].astype(F32)).astype(BF16)
    gu_ref[...] = gu
    dbu_ref[...] = col_sum(gu)
    part = nt(gu, wu_ref[...])

    @pl.when(j == 0)
    def _():
        acc[...] = part

    @pl.when(j > 0)
    def _():
        acc[...] += part

    @pl.when(j == pl.num_programs(0) - 1)
    def _():
        for copy in copies:
            copy.wait()
        gn = acc[...]
        u, r = unit(a_ref[...])
        g = g_ref[...].astype(F32)
        ga = g + norm_back(gn, u, r, gain_ref[...].astype(F32))
        ga_ref[...] = ga
        gt = ga.astype(BF16)
        gt_ref[...] = gt
        gc_ref[...] = nt(gt, wo_ref[...]).astype(BF16)
        sm_ref[0:1, :] = col_sum(gn * u)
        sm_ref[1:2, :] = col_sum(gn)
        sm_ref[2:3, :] = col_sum(g)
        sm_ref[3:4, :] = col_sum(gt)


def mlp_back(at, g, gp, w, after, gain, slot, slots, owners, prev, wait=()):
    s, d = g.shape
    n = gp.shape[2]
    t = n // owners
    row = fixed((None, s, d), (slot, 0, 0))
    anywhere = pl.BlockSpec(memory_space=pl.ANY)
    return call(
        mlp_back_kernel,
        "mlp_back",
        (owners,),
        [
            (g, fixed((s, d))),
            (gp, spec((None, s, t), lambda j, r: (r[0], 0, j))),
            (w, spec((d, t), lambda j, r: (0, 4 * d // t + j))),
            (gain, fixed((1, d))),
            (after, anywhere),
            (w, anywhere),
        ]
        + down_blocks(w, owners, n // d),
        [
            ((slots, s, n), BF16, spec((None, s, t), lambda j, r: (slot, 0, j))),
            ((s, d), F32, fixed((s, d))),
            ((slots, s, d), BF16, row),
            ((s, d), BF16, fixed((s, d))),
            ((slots, 1, n), F32, spec((None, 1, t), lambda j, r: (slot, 0, j))),
            ((slots, 4, d), F32, fixed((None, 4, d), (slot, 0, 0))),
        ],
        scratch=[
            pltpu.VMEM((s, d), F32),
            pltpu.VMEM((s, d), F32),
            pltpu.VMEM((d, d), BF16),
            pltpu.SemaphoreType.DMA((2,)),
        ],
        scalars=at,
        prev=prev,
        wait=wait,
        flops=4 * s * d * n + 2 * s * d * d,
    )


def attend_back(q, k, v, do, logs):
    scale = LOG2E * HEAD_DIM**-0.5
    heads = head_slices(q.shape[1] // HEAD_DIM)
    kt, qt, dot = k.T, q.T, do.T
    scores = [nt(k[:, at], q[:, at]) for at in heads]
    dps = [nt(v[:, at], do[:, at]) for at in heads]
    dqs, dks, dvs = [], [], []
    for h, at in enumerate(heads):
        p = jnp.exp2(scores[h] * scale - logs[h])
        pdp = p * dps[h]
        ds = (pdp - p * jnp.sum(pdp, axis=0, keepdims=True)).astype(BF16)
        dvs.append(nt(dot[at], p.astype(BF16)).astype(BF16))
        dks.append((nt(qt[at], ds) * HEAD_DIM**-0.5).astype(BF16))
        dqs.append((nn(kt[at], ds) * HEAD_DIM**-0.5).astype(BF16))
    return [jnp.concatenate(pieces, axis=0) for pieces in (dqs, dks, dvs)]


def attn_back_kernel(at_ref, q_ref, k_ref, v_ref, do_ref, l_ref, o_ref):
    lanes = q_ref.shape[1]
    count = lanes // HEAD_DIM
    j = pl.program_id(0)
    first_head = lax.rem(j, l_ref.shape[0] // count) * count
    logs = [l_ref[pl.ds(first_head + h, 1), :] for h in range(count)]
    d = o_ref.shape[1] // 3
    grads = attend_back(q_ref[...], k_ref[...], v_ref[...], do_ref[...], logs)
    for part, grad in enumerate(grads):
        first = pl.multiple_of(part * d + j * lanes, lanes)
        o_ref[:, pl.ds(first, lanes)] = grad.T


def attn_back(at, qkv, gc, logs, slot, slots, prev, wait=()):
    _, s, n = qkv.shape
    d = n // 3
    lanes = BACK_HEADS * HEAD_DIM
    groups = d // lanes
    ratio = FORWARD_HEADS // BACK_HEADS

    def block(part):
        return spec((None, s, lanes), lambda j, r: (r[0], 0, j + part * groups))

    return call(
        attn_back_kernel,
        "attn_back",
        (groups,),
        [
            (qkv, block(0)),
            (qkv, block(1)),
            (qkv, block(2)),
            (gc, spec((s, lanes), lambda j, r: (0, j))),
            (
                logs,
                spec((None, None, FORWARD_HEADS, s), lambda j, r: (r[0], j // ratio, 0, 0)),
            ),
        ],
        [((slots, s, n), BF16, fixed((None, s, n), (slot, 0, 0)))],
        scalars=at,
        prev=prev,
        wait=wait,
        flops=10 * s * s * d * 3,
    )[0]


def qkv_back_kernel(at_ref, g_ref, w_ref, x_ref, ga_ref, gain_ref, o_ref, ob_ref, sm_ref):
    d = x_ref.shape[1]
    gn = nt(g_ref[...], w_ref[...])
    u, r = unit(x_ref[...].astype(F32))
    out = ga_ref[...] + norm_back(gn, u, r, gain_ref[...].astype(F32))
    o_ref[...] = out
    ob_ref[...] = out.astype(BF16)
    sm_ref[0:1, :] = col_sum(gn * u)
    sm_ref[1:2, :] = col_sum(gn)
    sm_ref[2:3, :] = col_sum(g_ref[:, 0:d])
    sm_ref[3:4, :] = col_sum(g_ref[:, 2 * d : 3 * d])


def qkv_back(at, gqkv, w, xb, ga, gain, slot, prev, wait=()):
    slots, s, n = gqkv.shape
    d = n // 3
    return call(
        qkv_back_kernel,
        "qkv_back",
        (1,),
        [
            (gqkv, fixed((None, s, n), (slot, 0, 0))),
            (w, fixed((d, n))),
            (xb, spec((None, s, d), lambda j, r: (r[0], 0, 0))),
            (ga, fixed((s, d))),
            (gain, fixed((1, d))),
        ],
        [
            ((s, d), F32, fixed((s, d))),
            ((s, d), BF16, fixed((s, d))),
            ((slots, 4, d), F32, fixed((None, 4, d), (slot, 0, 0))),
        ],
        scalars=at,
        prev=prev,
        wait=wait,
        flops=2 * s * d * n,
    )


def back_kernel(slot, owners, at_ref, g_ref, gp_ref, wu_ref, gain2_ref, gain1_ref, *refs):
    q_ref, k_ref, v_ref, l_ref, wq_ref, a_hbm, w_hbm, x_hbm = refs[:8]
    blocks = refs[8:-20]
    (
        gu_ref, gt_hbm, gqkv_hbm, dbu_ref, sm2_ref, grad_ref, low_ref, sm1_ref,
        acc, a_ref, wo_ref, x_ref, ga_ref, gt_ref, gc_ref, gqkv_ref, gn_ref, sems, sems_out, _,
    ) = refs[-20:]
    j = pl.program_id(0)
    s, d = g_ref.shape
    lanes = q_ref.shape[1]
    groups = d // lanes
    last = pl.num_programs(0) - 1
    reads = (
        pltpu.make_async_copy(a_hbm.at[at_ref[0]], a_ref, sems.at[0]),
        pltpu.make_async_copy(w_hbm.at[:, pl.ds(3 * d, d)], wo_ref, sems.at[1]),
        pltpu.make_async_copy(x_hbm.at[at_ref[0]], x_ref, sems.at[2]),
    )
    writes = (
        pltpu.make_async_copy(gt_ref, gt_hbm.at[slot], sems_out.at[0]),
        pltpu.make_async_copy(gqkv_ref, gqkv_hbm.at[slot], sems_out.at[1]),
    )

    @pl.when(j == 0)
    def _():
        for copy in reads:
            copy.start()

    @pl.when(j < owners)
    def _():
        gh = jnp.concatenate([nt(g_ref[...], block[...]) for block in blocks], axis=1)
        gu = (gh * gp_ref[...].astype(F32)).astype(BF16)
        gu_ref[...] = gu
        dbu_ref[...] = col_sum(gu)
        part = nt(gu, wu_ref[...])

        @pl.when(j == 0)
        def _():
            acc[...] = part

        @pl.when(j > 0)
        def _():
            acc[...] += part

    @pl.when(j == owners - 1)
    def _():
        for copy in reads:
            copy.wait()
        gn = acc[...]
        u, r = unit(a_ref[...])
        g = g_ref[...].astype(F32)
        ga = g + norm_back(gn, u, r, gain2_ref[...].astype(F32))
        ga_ref[...] = ga
        gt = ga.astype(BF16)
        gt_ref[...] = gt
        writes[0].start()
        gc_ref[...] = nt(gt, wo_ref[...]).astype(BF16)
        sm2_ref[0:1, :] = col_sum(gn * u)
        sm2_ref[1:2, :] = col_sum(gn)
        sm2_ref[2:3, :] = col_sum(g)
        sm2_ref[3:4, :] = col_sum(gt)

    @pl.when((j >= owners) & (j < owners + groups))
    def _():
        group = j - owners
        count = lanes // HEAD_DIM
        first_head = lax.rem(group, l_ref.shape[0] // count) * count
        logs = [l_ref[pl.ds(first_head + h, 1), :] for h in range(count)]
        do = gc_ref[:, pl.ds(pl.multiple_of(group * lanes, lanes), lanes)]
        grads = attend_back(q_ref[...], k_ref[...], v_ref[...], do, logs)
        for part, grad in enumerate(grads):
            first = pl.multiple_of(part * d + group * lanes, lanes)
            gqkv_ref[:, pl.ds(first, lanes)] = grad.T

    @pl.when(j >= owners + groups)
    def _():
        part = j - owners - groups
        columns = gqkv_ref[:, pl.ds(pl.multiple_of(part * d, d), d)]
        product = nt(columns, wq_ref[...])

        @pl.when(part == 0)
        def _():
            writes[1].start()
            gn_ref[...] = product
            sm1_ref[2:3, :] = col_sum(columns)

        @pl.when(part > 0)
        def _():
            gn_ref[...] += product

        @pl.when(j == last)
        def _():
            sm1_ref[3:4, :] = col_sum(columns)
            gn = gn_ref[...]
            u, r = unit(x_ref[...].astype(F32))
            out = ga_ref[...] + norm_back(gn, u, r, gain1_ref[...].astype(F32))
            grad_ref[...] = out
            low_ref[...] = out.astype(BF16)
            sm1_ref[0:1, :] = col_sum(gn * u)
            sm1_ref[1:2, :] = col_sum(gn)
            for copy in writes:
                copy.wait()


def back(at, g, w, kept, gain1, gain2, slot, slots, owners, prev):
    xb, _, qkv, _, logs, after, _, _, gp = kept
    s, d = g.shape
    n = gp.shape[2]
    t = n // owners
    lanes = BACK_HEADS * HEAD_DIM
    groups = d // lanes
    ratio = FORWARD_HEADS // BACK_HEADS
    anywhere = pl.BlockSpec(memory_space=pl.ANY)

    def owner(j):
        return jnp.minimum(j, owners - 1)

    def group(j):
        return jnp.clip(j - owners, 0, groups - 1)

    def heads(part):
        return spec((None, s, lanes), lambda j, r: (r[0], 0, group(j) + part * groups))

    def down_block(k):
        return (w, spec((d // owners, d), lambda j, r: (owner(j), 8 + k)))

    return call(
        partial(back_kernel, slot, owners),
        "back",
        (owners + groups + 3,),
        [
            (g, fixed((s, d))),
            (gp, spec((None, s, t), lambda j, r: (r[0], 0, owner(j)))),
            (w, spec((d, t), lambda j, r: (0, 4 * d // t + owner(j)))),
            (gain2, fixed((1, d))),
            (gain1, fixed((1, d))),
            (qkv, heads(0)),
            (qkv, heads(1)),
            (qkv, heads(2)),
            (
                logs,
                spec(
                    (None, None, FORWARD_HEADS, s), lambda j, r: (r[0], group(j) // ratio, 0, 0)
                ),
            ),
            (w, spec((d, d), lambda j, r: (0, jnp.clip(j - owners - groups, 0, 2)))),
            (after, anywhere),
            (w, anywhere),
            (xb, anywhere),
        ]
        + [down_block(k) for k in range(n // d)],
        [
            ((slots, s, n), BF16, spec((None, s, t), lambda j, r: (slot, 0, owner(j)))),
            ((slots, s, d), BF16, anywhere),
            ((slots, s, 3 * d), BF16, anywhere),
            ((slots, 1, n), F32, spec((None, 1, t), lambda j, r: (slot, 0, owner(j)))),
            ((slots, 4, d), F32, fixed((None, 4, d), (slot, 0, 0))),
            ((s, d), F32, fixed((s, d))),
            ((s, d), BF16, fixed((s, d))),
            ((slots, 4, d), F32, fixed((None, 4, d), (slot, 0, 0))),
        ],
        scratch=[
            pltpu.VMEM((s, d), F32),
            pltpu.VMEM((s, d), F32),
            pltpu.VMEM((d, d), BF16),
            pltpu.VMEM((s, d), BF16),
            pltpu.VMEM((s, d), F32),
            pltpu.VMEM((s, d), BF16),
            pltpu.VMEM((s, d), BF16),
            pltpu.VMEM((s, 3 * d), BF16),
            pltpu.VMEM((s, d), F32),
            pltpu.SemaphoreType.DMA((3,)),
            pltpu.SemaphoreType.DMA((2,)),
            pltpu.VMEM((8, 128), F32),
        ],
        scalars=at,
        prev=prev,
        flops=4 * s * d * n + 8 * s * d * d + 30 * s * s * d,
    )


def weight_grad_kernel(at_ref, a_ref, b0_ref, b1_ref, send_ref, keep_ref, left, right):
    s = b0_ref.shape[0]
    step = right.shape[0] // 2
    i = pl.program_id(0)

    @pl.when(i == 0)
    def _():
        right[...] = jnp.zeros_like(right)
        left[...] = jnp.zeros_like(left)
        for image in range(2):
            left[:, image * step : image * step + s] = a_ref[image].T

    right[0:s, :] = b0_ref[...]
    right[step : step + s, :] = b1_ref[...]
    owners, rows, cols = send_ref.shape
    out = nn(left[...], right[...]).astype(BF16).reshape(owners, rows, cols)

    @pl.when(i < pl.num_programs(0) // 2)
    def _():
        send_ref[...] = out

    @pl.when(i >= pl.num_programs(0) // 2)
    def _():
        keep_ref[...] = out


def weight_grad(at, left, right, owners, replicas, name, wait=()):
    _, s, m = left.shape
    n = right.shape[2]
    chips = replicas // CORES
    rows, cols = m // owners, n // replicas
    step = -(-s // 128) * 128

    def col(image):
        def index(i, r):
            core = jnp.where(i < chips, 1 - r[2], r[2])
            return (r[1] + image, 0, lax.rem(i, chips) * CORES + core)

        return spec((None, s, cols), index)

    def out(first):
        return (
            (chips, owners, rows, cols),
            BF16,
            spec(
                (None, owners, rows, cols),
                lambda i, r: (jnp.clip(i - first, 0, chips - 1), 0, 0, 0),
            ),
        )

    return call(
        weight_grad_kernel,
        name,
        (replicas,),
        [
            (left, spec((2, s, m), lambda i, r: (r[0], 0, 0))),
            (right, col(0)),
            (right, col(1)),
        ],
        [out(0), out(chips)],
        scratch=[pltpu.VMEM((m, 2 * step), BF16), pltpu.VMEM((2 * step, cols), BF16)],
        scalars=at,
        wait=wait,
        flops=4 * s * m * n,
    )


class Place:
    def __init__(self):
        self.owners = lax.axis_size("shard")
        self.replicas = lax.axis_size("rep")
        self.chips = self.replicas // CORES
        self.z = lax.axis_index("shard")
        rep = lax.axis_index("rep")
        self.rep = rep
        self.y = rep // CORES
        self.core = rep % CORES

    def ring_z(self, block, step=1):
        n = self.owners
        return lax.ppermute(block, "shard", [(i, (i + step) % n) for i in range(n)])

    def ring_y(self, block):
        n = self.chips
        route = [
            (y * CORES + c, ((y + 1) % n) * CORES + c) for y in range(n) for c in range(CORES)
        ]
        return lax.ppermute(block, "rep", route)

    def swap_core(self, block):
        route = [(i, i ^ 1) for i in range(self.replicas)]
        return lax.ppermute(block, "rep", route)


def gather_vector(place, vector):
    held = [vector] + [place.ring_z(vector, step) for step in range(1, place.owners)]
    order = lax.rem(place.z - jnp.arange(place.owners) + place.owners, place.owners)
    return jnp.take(jnp.stack(held), order, axis=0)


def zero_after(value):
    corner = lax.slice(value, (0,) * value.ndim, (1,) * value.ndim)
    return (corner.reshape(()).astype(F32) * 0.0).astype(jnp.int32)


def gather_weights(place, w_qkv, w_out, w_up, w_down):
    rows, d = w_out.shape
    part = rows // place.replicas
    first = place.rep * part
    blocks = [w_down[k : k + rows] for k in range(0, w_down.shape[0], rows)]
    whole = jnp.concatenate([w_qkv, w_out, w_up] + blocks, axis=1)
    mine = lax.dynamic_slice_in_dim(whole, first, part, 0)
    return lax.all_gather(mine, ("shard", "rep"), axis=0, tiled=True)


def add(*terms):
    total = terms[0].astype(F32)
    for term in terms[1:]:
        total = total + term.astype(F32)
    return total.astype(BF16)


def pick(holder, index, axis):
    return lax.dynamic_index_in_dim(holder, index, axis, keepdims=False)


def finish_kernel(count, at_ref, *refs):
    pieces, out_ref = refs[:count], refs[-1]
    for i, piece in enumerate(pieces):
        cols = piece.shape[1]
        first = pl.multiple_of(at_ref[i] * cols, cols)
        out_ref[:, pl.ds(first, cols)] = piece[...].astype(F32)


def finish(pieces, parts, wait=()):
    rows, cols = pieces[0].shape
    whole = pl.BlockSpec(memory_space=pltpu.VMEM)
    out = pl.pallas_call(
        partial(finish_kernel, len(pieces)),
        in_specs=[pl.BlockSpec(memory_space=pltpu.SMEM)]
        + [whole] * len(pieces)
        + [pl.BlockSpec(memory_space=pl.ANY)] * len(wait),
        out_specs=whole,
        out_shape=jax.ShapeDtypeStruct((rows, cols * len(pieces)), F32),
        compiler_params=pltpu.CompilerParams(vmem_limit_bytes=VMEM_BYTES),
        cost_estimate=pl.CostEstimate(
            flops=0, bytes_accessed=0, transcendentals=0
        ),
        name="finish",
    )(jnp.stack(parts).astype(jnp.int32), *pieces, *wait)
    return out[None]


def reduce_chips(place, held, *earlier):
    chips = place.chips
    late = [zero_after(value) for value in earlier]
    total = pick(held, lax.rem(place.y + chips - 1, chips), 0)
    for step in range(1, chips):
        total = add(
            place.ring_y(total),
            pick(held, lax.rem(place.y + 2 * chips - 1 - step, chips), 0),
            *late,
        )
    return total


def reduce_rows(place, held, *wait):
    total = lax.psum_scatter(held, "shard", scatter_dimension=0, tiled=True)[0]
    chips = place.chips
    pieces, parts = [], []
    for t in range(chips):
        if t > 0:
            total = place.ring_y(total)
        chip = lax.rem(place.y - t + chips, chips)
        pieces += [total, place.swap_core(total)]
        parts += [chip * CORES + place.core, chip * CORES + 1 - place.core]
    return finish(pieces, parts, wait)


def sum_small(place, table):
    total = table + place.swap_core(table)
    ring = total
    for _ in range(1, place.chips):
        ring = place.ring_y(ring)
        total = total + ring
    owners = place.owners
    out = pick(total, place.z, 0)
    for step in range(1, owners):
        out = out + place.ring_z(pick(total, lax.rem(place.z + step, owners), 0), step)
    return out[None]


def per_device(
    images, cotangent, ln1_scale, ln1_shift, w_qkv, bias_qv, w_out, bias_out,
    ln2_scale, ln2_shift, w_up, bias_up, w_down, bias_down,
):
    place = Place()
    section = lax.axis_index("section")
    first = section == 0
    _, s, d = images.shape

    given = (
        ln1_scale, ln1_shift, bias_qv, bias_out, ln2_scale, ln2_shift, bias_up, bias_down
    )
    widths = [v.shape[1] for v in given]
    packed = gather_vector(place, jnp.concatenate(given, axis=1)[0])
    w = gather_weights(place, w_qkv[0], w_out[0], w_up[0], w_down[0])

    whole = []
    start = 0
    for width in widths:
        whole.append(packed[:, start : start + width].reshape(1, -1))
        start += width
    gain1, shift1, bias_two, bias_o, gain2, shift2, bias_u, bias_d = whole
    bias_mixed = jnp.concatenate(
        [bias_two[:, :d], jnp.zeros((1, d), BF16), bias_two[:, d:]], axis=1
    )
    slots = 4

    def send_on(block):
        return lax.ppermute(block, "section", [(0, 1)])

    def send_back(block):
        return lax.ppermute(block, "section", [(1, 0)])

    vectors = (gain1, shift1, bias_mixed, bias_o, gain2, shift2, bias_u, bias_d)
    kept = (None,) * 9

    def forward(x, slot, with_down):
        nonlocal kept
        results = front(x, w, vectors, slot, slots, place.owners, kept, with_down)
        kept = tuple(results[:9])
        return results[9] if with_down else None

    def forward_down(slot, *earlier):
        return down(hidden, w, after, bias_d, slot, place.owners, earlier)

    gslots = 3
    gu = gt = gqkv = dbu = sm2 = sm1 = None

    def back_mlp(source, upstream, slot, *wait):
        nonlocal gu, gt, dbu, sm2
        gu, ga, gt, gc, dbu, sm2 = mlp_back(
            source, upstream, gp, w, after, gain2, slot, gslots, place.owners,
            (gu, None, gt, None, dbu, sm2), wait,
        )
        return ga, gc

    def back_attn(source, gc, slot, *wait):
        nonlocal gqkv
        gqkv = attn_back(source, qkv, gc, logs, slot, gslots, (gqkv,), wait)

    def back_qkv(source, ga, slot, *wait):
        nonlocal sm1
        grad, low, sm1 = qkv_back(source, gqkv, w, xb, ga, gain1, slot, (None, None, sm1), wait)
        return grad, low

    def back_all(source, upstream, slot):
        nonlocal gu, gt, gqkv, dbu, sm2, sm1
        gu, gt, gqkv, dbu, sm2, grad, low, sm1 = back(
            source, upstream, w, kept, gain1, gain2, slot, gslots, place.owners,
            (gu, gt, gqkv, dbu, sm2, None, None, sm1),
        )
        return grad, low

    def source_slot(value):
        return jnp.asarray(value, jnp.int32).reshape(1)

    out0 = forward(images[0], 0, True)
    arrived0 = send_on(out0)
    out1 = forward(images[1], 1, True)
    arrived1 = send_on(out1)
    forward(arrived0, 2, False)
    xb, n1, qkv, ctx, logs, after, n2, hidden, gp = kept
    source = source_slot(2)
    up0 = cotangent[0]
    grad0, low0 = back_all(source, up0, 0)
    returned0 = send_back(low0)

    forward(arrived1, 3, False)
    xb, n1, qkv, ctx, logs, after, n2, hidden, gp = kept
    source = source_slot(jnp.where(first, 0, 3))
    up1 = jnp.where(first, returned0, cotangent[1])
    grad1, low1 = back_all(source, up1, 1)
    up2 = send_back(low1)

    out2 = forward_down(2, low1)
    out3 = forward_down(3, out2)
    section_out = jnp.where(first, jnp.stack([out0, out1]), jnp.stack([out2, out3]))
    at = jnp.stack([section, 1 - section, place.core]).astype(jnp.int32)

    sizes = (place.owners, place.replicas)

    def products(left, right, name, *earlier):
        sent, kept = weight_grad(at, left, right, *sizes, name, earlier)
        return add(kept, place.swap_core(sent))

    source = source_slot(1)
    h_down = products(hidden, jnp.stack([up0, up1, up2]), "dw_down", out2, out3)
    t_down = reduce_chips(place, h_down)
    ga, gc = back_mlp(source, up2, 2, h_down)
    h_up = products(n2, gu, "dw_up")
    t_up = reduce_chips(place, h_up)
    h_out = products(ctx, gt, "dw_out", t_down)
    t_out = reduce_chips(place, h_out)
    back_attn(source, gc, 2, h_out, h_up)
    h_qkv = products(n1, gqkv, "dw_qkv")
    t_qkv = reduce_chips(place, h_qkv)
    grad2, low2 = back_qkv(source, ga, 2, h_qkv, t_up)

    grad_in = jnp.where(
        first,
        jnp.stack([grad1, grad2]),
        jnp.stack([low0.astype(F32), low1.astype(F32)]),
    )
    gw_down = reduce_rows(place, t_down)
    gw_up = reduce_rows(place, t_up)
    gw_out = reduce_rows(place, t_out)
    gw_qkv = reduce_rows(place, t_qkv, gw_down, gw_up, gw_out, grad_in, section_out)

    def own(holder):
        pair = lax.dynamic_slice_in_dim(holder, 1 - section, 2, 0)
        return jnp.sum(pair, axis=0)

    sm1, sm2, dbu = own(sm1), own(sm2), own(dbu)
    smalls = (
        sm1[0:1], sm1[1:2], jnp.concatenate([sm1[2:3], sm1[3:4]], axis=1), sm2[3:4],
        sm2[0:1], sm2[1:2], dbu, sm2[2:3],
    )
    table = jnp.concatenate([v.reshape(place.owners, -1) for v in smalls], axis=1)
    mine = sum_small(place, table)
    shares = []
    start = 0
    for width in widths:
        shares.append(mine[:, start : start + width])
        start += width
    (g_ln1s, g_ln1b, g_bqv, g_bo, g_ln2s, g_ln2b, g_bu, g_bd) = shares
    return (
        section_out[None], grad_in[None], g_ln1s, g_ln1b, gw_qkv, g_bqv, gw_out, g_bo,
        g_ln2s, g_ln2b, gw_up, g_bu, gw_down, g_bd,
    )


def solution(mesh):
    batch = P(("shard", "rep"), None, None)
    layers = P("section", ("shard", "rep"), None, None)
    vec = P("section", "shard")
    mat = P("section", "shard", None)
    in_specs = (
        batch, batch, vec, vec, mat, vec, mat, vec, vec, vec, mat, vec, mat, vec
    )
    out_specs = (
        layers, layers, vec, vec, mat, vec, mat, vec, vec, vec, mat, vec, mat, vec
    )
    return jax.shard_map(
        per_device, mesh=mesh, in_specs=in_specs, out_specs=out_specs, check_vma=False
    )
```

```python
from functools import partial

import jax
import jax.numpy as jnp
from jax import lax
from jax.experimental import pallas as pl
from jax.experimental.pallas import tpu as pltpu
from jax.sharding import PartitionSpec as P

HEAD_DIM = 64
CORES = 2
NORM_EPSILON = 1e-06
LOG2E = 1.4426950408889634
VMEM_BYTES = 56 * 1024 * 1024
F32 = jnp.float32
BF16 = jnp.bfloat16
COST = 4


def nn(left, right):
    return jnp.dot(left, right, preferred_element_type=F32)


def nt(left, right):
    return lax.dot_general(left, right, (((1,), (1,)), ((), ())), preferred_element_type=F32)


def tn(left, right):
    return lax.dot_general(left, right, (((0,), (0,)), ((), ())), preferred_element_type=F32)


def unit(values):
    centred = values - jnp.mean(values, axis=-1, keepdims=True)
    inv = lax.rsqrt(jnp.mean(centred * centred, axis=-1, keepdims=True) + NORM_EPSILON)
    return centred * inv, inv


def norm_back(grad, unit_rows, inv, gain):
    e = grad * gain
    return inv * (
        e
        - jnp.mean(e, axis=-1, keepdims=True)
        - unit_rows * jnp.mean(e * unit_rows, axis=-1, keepdims=True)
    )


def col_sum(values):
    return jnp.sum(values.astype(F32), axis=0, keepdims=True)


def gelu_parts(x):
    cdf = 0.5 + 0.5 * lax.erf(x * 0.7071067811865476)
    return x * cdf, cdf + x * (jnp.exp2(x * x * (-0.5 * LOG2E)) * 0.3989422804014327)


def spec(shape, index):
    return pl.BlockSpec(shape, index)


def fixed(shape, at=None):
    at = (0,) * len(shape) if at is None else at
    return pl.BlockSpec(shape, lambda *_: at)


def call(kernel, name, grid, ins, outs, scratch=(), scalars=None, prev=None, wait=(), flops=0):
    arrays = [a for a, _ in ins]
    in_specs = [s for _, s in ins]
    body = kernel
    if len(wait) > 0:
        read, prev = len(ins) + (scalars is not None), prev or [None] * len(outs)
        arrays += list(wait)
        in_specs += [pl.BlockSpec(memory_space=pl.ANY)] * len(wait)
        ins = list(ins) + [(w, None) for w in wait]
        inner = kernel

        def kernel(*refs):
            inner(*refs[:read], *refs[read + len(wait) :])

        body = kernel
    aliases = {}
    n_scalar = 0 if scalars is None else 1
    if prev is not None:
        count = len(ins)
        held = [(i, p) for i, p in enumerate(prev) if p is not None]
        for k, (i, p) in enumerate(held):
            aliases[n_scalar + count + k] = i
            arrays.append(p)
            in_specs.append(pl.BlockSpec(memory_space=pl.ANY))

        def body(*refs):
            kernel(*refs[: n_scalar + count], *refs[n_scalar + count + len(held) :])

    cost = pl.CostEstimate(flops=int(flops * COST), bytes_accessed=0, transcendentals=0)
    params = pltpu.CompilerParams(
        dimension_semantics=("arbitrary",) * len(grid), vmem_limit_bytes=VMEM_BYTES
    )
    out_shape = [jax.ShapeDtypeStruct(s, d) for s, d, _ in outs]
    out_specs = [s for _, _, s in outs]
    if scalars is None:
        f = pl.pallas_call(
            body,
            grid=grid,
            in_specs=in_specs,
            out_specs=out_specs,
            out_shape=out_shape,
            scratch_shapes=list(scratch),
            input_output_aliases=aliases,
            compiler_params=params,
            cost_estimate=cost,
            name=name,
        )
        return f(*arrays)
    f = pl.pallas_call(
        body,
        grid_spec=pltpu.PrefetchScalarGridSpec(
            num_scalar_prefetch=1,
            grid=grid,
            in_specs=in_specs,
            out_specs=out_specs,
            scratch_shapes=list(scratch),
        ),
        out_shape=out_shape,
        input_output_aliases=aliases,
        compiler_params=params,
        cost_estimate=cost,
        name=name,
    )
    return f(scalars, *arrays)


def head_slices(count):
    return [slice(h * HEAD_DIM, (h + 1) * HEAD_DIM) for h in range(count)]


def attend(q, k, v):
    scale = LOG2E * HEAD_DIM**-0.5
    heads = head_slices(q.shape[1] // HEAD_DIM)
    values = v.T
    scores = [nt(k[:, at], q[:, at]) for at in heads]
    outs, logs = [], []
    for h, at in enumerate(heads):
        top = jnp.max(scores[h], axis=0, keepdims=True)
        p = jnp.exp2((scores[h] - top) * scale)
        total = jnp.sum(p, axis=0, keepdims=True)
        outs.append((nn(values[at], p.astype(BF16)) * (1.0 / total)).astype(BF16))
        logs.append(top * scale + jnp.log2(total))
    return jnp.concatenate(outs, axis=0).T, logs


FORWARD_HEADS = 4
BACK_HEADS = 2


def down_blocks(w, owners, count):
    d = w.shape[0]

    def block(k):
        return (w, spec((d // owners, d), lambda j, *_: (j, 8 + k)))

    return [block(k) for k in range(count)]


def down_kernel(h_ref, *refs):
    blocks, (a_ref, b_ref, o_ref, acc) = refs[:-4], refs[-4:]
    j = pl.program_id(0)
    rows = blocks[0].shape[0]
    part = sum(nn(h_ref[:, k * rows : (k + 1) * rows], b[...]) for k, b in enumerate(blocks))

    @pl.when(j == 0)
    def _():
        acc[...] = a_ref[...] + b_ref[...].astype(F32) + part

    @pl.when(j > 0)
    def _():
        acc[...] += part

    @pl.when(j == pl.num_programs(0) - 1)
    def _():
        o_ref[...] = acc[...].astype(BF16)


def down(hidden, w, after, bias, slot, owners, wait=()):
    _, s, n = hidden.shape
    d = w.shape[0]
    t = n // owners
    return call(
        down_kernel,
        "down",
        (owners,),
        [(hidden, spec((None, s, t), lambda j: (slot, 0, j)))]
        + down_blocks(w, owners, n // d)
        + [(after, fixed((None, s, d), (slot, 0, 0))), (bias, fixed((1, d)))],
        [((s, d), BF16, fixed((s, d)))],
        scratch=[pltpu.VMEM((s, d), F32)],
        wait=wait,
        flops=2 * s * d * n,
    )[0]


UP_TILE = 512


def front_kernel(slot, count, *refs):
    (x_ref, g1_ref, s1_ref, w_ref, bq_ref, bo_ref, g2_ref, s2_ref, wu_ref, bu_ref) = refs[:10]
    blocks = refs[10 : 10 + count]
    rest = refs[10 + count :]
    if count > 0:
        bd_ref, rest = rest[0], rest[1:]
    outs, (h_ref, gp_ref), rest = rest[:7], rest[7:9], rest[9:]
    if count > 0:
        out_ref, rest = rest[0], rest[1:]
    n1_ref, qkv_ref, ctx_ref, logs_ref, a_ref, n2_ref, sems = rest[:7]
    j = pl.program_id(0)
    d = x_ref.shape[1]
    groups = logs_ref.shape[0]
    lanes = d // groups
    out_step = 3 + groups
    ups = 4 * d // UP_TILE
    copies = [
        pltpu.make_async_copy(ref, out.at[slot], sems.at[i])
        for i, (ref, out) in enumerate(
            zip((x_ref, n1_ref, qkv_ref, ctx_ref, logs_ref, a_ref, n2_ref), outs)
        )
    ]

    @pl.when(j == 0)
    def _():
        u, _ = unit(x_ref[...].astype(F32))
        n1_ref[...] = (u * g1_ref[...].astype(F32) + s1_ref[...].astype(F32)).astype(BF16)
        copies[0].start()
        copies[1].start()

    @pl.when(j < 3)
    def _():
        first = pl.multiple_of(j * d, d)
        qkv_ref[:, pl.ds(first, d)] = (
            nn(n1_ref[...], w_ref[...]) + bq_ref[...].astype(F32)
        ).astype(BF16)

    @pl.when(j == 2)
    def _():
        copies[2].start()

    @pl.when((j >= 3) & (j < out_step))
    def _():
        group = j - 3
        q, k, v = [
            qkv_ref[:, pl.ds(pl.multiple_of(part * d + group * lanes, lanes), lanes)]
            for part in range(3)
        ]
        ctx, logs = attend(q, k, v)
        ctx_ref[:, pl.ds(pl.multiple_of(group * lanes, lanes), lanes)] = ctx
        for h, log in enumerate(logs):
            logs_ref[group, h : h + 1, :] = log

    @pl.when(j == out_step)
    def _():
        copies[3].start()
        copies[4].start()
        a = x_ref[...].astype(F32) + (nn(ctx_ref[...], w_ref[...]) + bo_ref[...].astype(F32))
        a_ref[...] = a
        u, _ = unit(a)
        n2_ref[...] = (u * g2_ref[...].astype(F32) + s2_ref[...].astype(F32)).astype(BF16)
        copies[5].start()
        copies[6].start()

    @pl.when((j > out_step) & (j <= out_step + ups))
    def _():
        h, gp = gelu_parts(nn(n2_ref[...], wu_ref[...]) + bu_ref[...].astype(F32))
        h = h.astype(BF16)
        h_ref[...] = h
        gp_ref[...] = gp.astype(BF16)
        if count > 0:
            first = pl.multiple_of((j - out_step - 1) * UP_TILE, UP_TILE)
            rest[7][:, pl.ds(first, UP_TILE)] = h

    if count > 0:
        hidden, acc = rest[7], rest[8]

        @pl.when(j > out_step + ups)
        def _():
            owner = j - out_step - ups - 1
            rows = blocks[0].shape[0]
            part = sum(
                nn(
                    hidden[:, pl.ds(pl.multiple_of((owner * count + k) * rows, rows), rows)],
                    block[...],
                )
                for k, block in enumerate(blocks)
            )

            @pl.when(owner == 0)
            def _():
                acc[...] = a_ref[...] + bd_ref[...].astype(F32) + part

            @pl.when(owner > 0)
            def _():
                acc[...] += part

            @pl.when(j == pl.num_programs(0) - 1)
            def _():
                out_ref[...] = acc[...].astype(BF16)

    @pl.when(j == pl.num_programs(0) - 1)
    def _():
        for copy in copies:
            copy.wait()


def front(x, w, vectors, slot, slots, owners, prev, with_down):
    gain1, shift1, bias_q, bias_o, gain2, shift2, bias_u, bias_d = vectors
    s, d = x.shape
    n = bias_u.shape[1]
    groups = d // (FORWARD_HEADS * HEAD_DIM)
    first_up = 4 + groups
    ups = n // UP_TILE
    count = n // d if with_down else 0
    steps = first_up + ups + (owners if with_down else 0)

    def up_at(j):
        return jnp.clip(j - first_up, 0, ups - 1)

    def down_block(k):
        return (
            w,
            spec((d // owners, d), lambda j: (jnp.clip(j - first_up - ups, 0, owners - 1), 8 + k)),
        )

    vec = fixed((1, d))
    ins = [
        (x, fixed((s, d))),
        (gain1, vec),
        (shift1, vec),
        (w, spec((d, d), lambda j: (0, jnp.minimum(j, 3)))),
        (bias_q, spec((1, d), lambda j: (0, jnp.minimum(j, 2)))),
        (bias_o, vec),
        (gain2, vec),
        (shift2, vec),
        (w, spec((d, UP_TILE), lambda j: (0, 4 * d // UP_TILE + up_at(j)))),
        (bias_u, spec((1, UP_TILE), lambda j: (0, up_at(j)))),
    ] + [down_block(k) for k in range(count)]
    anywhere = pl.BlockSpec(memory_space=pl.ANY)
    tile = spec((None, s, UP_TILE), lambda j: (slot, 0, up_at(j)))
    outs = [
        ((slots, s, d), BF16, anywhere),
        ((slots, s, d), BF16, anywhere),
        ((slots, s, 3 * d), BF16, anywhere),
        ((slots, s, d), BF16, anywhere),
        ((slots, groups, FORWARD_HEADS, s), F32, anywhere),
        ((slots, s, d), F32, anywhere),
        ((slots, s, d), BF16, anywhere),
        ((slots, s, n), BF16, tile),
        ((slots, s, n), BF16, tile),
    ]
    scratch = [
        pltpu.VMEM((s, d), BF16),
        pltpu.VMEM((s, 3 * d), BF16),
        pltpu.VMEM((s, d), BF16),
        pltpu.VMEM((groups, FORWARD_HEADS, s), F32),
        pltpu.VMEM((s, d), F32),
        pltpu.VMEM((s, d), BF16),
        pltpu.SemaphoreType.DMA((7,)),
    ]
    prev = list(prev)
    if with_down:
        ins.append((bias_d, vec))
        outs.append(((s, d), BF16, fixed((s, d))))
        scratch += [pltpu.VMEM((s, n), BF16), pltpu.VMEM((s, d), F32)]
        prev.append(None)
    return call(
        partial(front_kernel, slot, count),
        "front",
        (steps,),
        ins,
        outs,
        scratch=scratch,
        prev=prev,
        flops=8 * s * d * d + 12 * s * s * d + 3 * s * d * n + (2 * s * d * n if with_down else 0),
    )


def mlp_back_kernel(at_ref, g_ref, gp_ref, wu_ref, gain_ref, a_hbm, wo_hbm, *refs):
    blocks, (gu_ref, ga_ref, gt_ref, gc_ref, dbu_ref, sm_ref, acc, a_ref, wo_ref, sems) = (
        refs[:-10],
        refs[-10:],
    )
    j = pl.program_id(0)
    d = a_ref.shape[1]
    copies = (
        pltpu.make_async_copy(a_hbm.at[at_ref[0]], a_ref, sems.at[0]),
        pltpu.make_async_copy(wo_hbm.at[:, pl.ds(3 * d, d)], wo_ref, sems.at[1]),
    )

    @pl.when(j == 0)
    def _():
        for copy in copies:
            copy.start()

    gh = jnp.concatenate([nt(g_ref[...], block[...]) for block in blocks], axis=1)
    gu = (gh * gp_ref[...].astype(F32)).astype(BF16)
    gu_ref[...] = gu
    dbu_ref[...] = col_sum(gu)
    part = nt(gu, wu_ref[...])

    @pl.when(j == 0)
    def _():
        acc[...] = part

    @pl.when(j > 0)
    def _():
        acc[...] += part

    @pl.when(j == pl.num_programs(0) - 1)
    def _():
        for copy in copies:
            copy.wait()
        gn = acc[...]
        u, r = unit(a_ref[...])
        g = g_ref[...].astype(F32)
        ga = g + norm_back(gn, u, r, gain_ref[...].astype(F32))
        ga_ref[...] = ga
        gt = ga.astype(BF16)
        gt_ref[...] = gt
        gc_ref[...] = nt(gt, wo_ref[...]).astype(BF16)
        sm_ref[0:1, :] = col_sum(gn * u)
        sm_ref[1:2, :] = col_sum(gn)
        sm_ref[2:3, :] = col_sum(g)
        sm_ref[3:4, :] = col_sum(gt)


def mlp_back(at, g, gp, w, after, gain, slot, slots, owners, prev, wait=()):
    s, d = g.shape
    n = gp.shape[2]
    t = n // owners
    row = fixed((None, s, d), (slot, 0, 0))
    anywhere = pl.BlockSpec(memory_space=pl.ANY)
    return call(
        mlp_back_kernel,
        "mlp_back",
        (owners,),
        [
            (g, fixed((s, d))),
            (gp, spec((None, s, t), lambda j, r: (r[0], 0, j))),
            (w, spec((d, t), lambda j, r: (0, 4 * d // t + j))),
            (gain, fixed((1, d))),
            (after, anywhere),
            (w, anywhere),
        ]
        + down_blocks(w, owners, n // d),
        [
            ((slots, s, n), BF16, spec((None, s, t), lambda j, r: (slot, 0, j))),
            ((s, d), F32, fixed((s, d))),
            ((slots, s, d), BF16, row),
            ((s, d), BF16, fixed((s, d))),
            ((slots, 1, n), F32, spec((None, 1, t), lambda j, r: (slot, 0, j))),
            ((slots, 4, d), F32, fixed((None, 4, d), (slot, 0, 0))),
        ],
        scratch=[
            pltpu.VMEM((s, d), F32),
            pltpu.VMEM((s, d), F32),
            pltpu.VMEM((d, d), BF16),
            pltpu.SemaphoreType.DMA((2,)),
        ],
        scalars=at,
        prev=prev,
        wait=wait,
        flops=4 * s * d * n + 2 * s * d * d,
    )


def attend_back(q, k, v, do, logs):
    scale = LOG2E * HEAD_DIM**-0.5
    heads = head_slices(q.shape[1] // HEAD_DIM)
    kt, qt, dot = k.T, q.T, do.T
    scores = [nt(k[:, at], q[:, at]) for at in heads]
    dps = [nt(v[:, at], do[:, at]) for at in heads]
    dqs, dks, dvs = [], [], []
    for h, at in enumerate(heads):
        p = jnp.exp2(scores[h] * scale - logs[h])
        pdp = p * dps[h]
        ds = (pdp - p * jnp.sum(pdp, axis=0, keepdims=True)).astype(BF16)
        dvs.append(nt(dot[at], p.astype(BF16)).astype(BF16))
        dks.append((nt(qt[at], ds) * HEAD_DIM**-0.5).astype(BF16))
        dqs.append((nn(kt[at], ds) * HEAD_DIM**-0.5).astype(BF16))
    return [jnp.concatenate(pieces, axis=0) for pieces in (dqs, dks, dvs)]


def attn_back_kernel(at_ref, q_ref, k_ref, v_ref, do_ref, l_ref, o_ref):
    lanes = q_ref.shape[1]
    count = lanes // HEAD_DIM
    j = pl.program_id(0)
    first_head = lax.rem(j, l_ref.shape[0] // count) * count
    logs = [l_ref[pl.ds(first_head + h, 1), :] for h in range(count)]
    d = o_ref.shape[1] // 3
    grads = attend_back(q_ref[...], k_ref[...], v_ref[...], do_ref[...], logs)
    for part, grad in enumerate(grads):
        first = pl.multiple_of(part * d + j * lanes, lanes)
        o_ref[:, pl.ds(first, lanes)] = grad.T


def attn_back(at, qkv, gc, logs, slot, slots, prev, wait=()):
    _, s, n = qkv.shape
    d = n // 3
    lanes = BACK_HEADS * HEAD_DIM
    groups = d // lanes
    ratio = FORWARD_HEADS // BACK_HEADS

    def block(part):
        return spec((None, s, lanes), lambda j, r: (r[0], 0, j + part * groups))

    return call(
        attn_back_kernel,
        "attn_back",
        (groups,),
        [
            (qkv, block(0)),
            (qkv, block(1)),
            (qkv, block(2)),
            (gc, spec((s, lanes), lambda j, r: (0, j))),
            (
                logs,
                spec((None, None, FORWARD_HEADS, s), lambda j, r: (r[0], j // ratio, 0, 0)),
            ),
        ],
        [((slots, s, n), BF16, fixed((None, s, n), (slot, 0, 0)))],
        scalars=at,
        prev=prev,
        wait=wait,
        flops=10 * s * s * d * 3,
    )[0]


def qkv_back_kernel(at_ref, g_ref, w_ref, x_ref, ga_ref, gain_ref, o_ref, ob_ref, sm_ref):
    d = x_ref.shape[1]
    gn = nt(g_ref[...], w_ref[...])
    u, r = unit(x_ref[...].astype(F32))
    out = ga_ref[...] + norm_back(gn, u, r, gain_ref[...].astype(F32))
    o_ref[...] = out
    ob_ref[...] = out.astype(BF16)
    sm_ref[0:1, :] = col_sum(gn * u)
    sm_ref[1:2, :] = col_sum(gn)
    sm_ref[2:3, :] = col_sum(g_ref[:, 0:d])
    sm_ref[3:4, :] = col_sum(g_ref[:, 2 * d : 3 * d])


def qkv_back(at, gqkv, w, xb, ga, gain, slot, prev, wait=()):
    slots, s, n = gqkv.shape
    d = n // 3
    return call(
        qkv_back_kernel,
        "qkv_back",
        (1,),
        [
            (gqkv, fixed((None, s, n), (slot, 0, 0))),
            (w, fixed((d, n))),
            (xb, spec((None, s, d), lambda j, r: (r[0], 0, 0))),
            (ga, fixed((s, d))),
            (gain, fixed((1, d))),
        ],
        [
            ((s, d), F32, fixed((s, d))),
            ((s, d), BF16, fixed((s, d))),
            ((slots, 4, d), F32, fixed((None, 4, d), (slot, 0, 0))),
        ],
        scalars=at,
        prev=prev,
        wait=wait,
        flops=2 * s * d * n,
    )


def back_kernel(slot, owners, at_ref, g_ref, gp_ref, wu_ref, gain2_ref, gain1_ref, *refs):
    q_ref, k_ref, v_ref, l_ref, wq_ref, a_hbm, w_hbm, x_hbm = refs[:8]
    blocks = refs[8:-20]
    (
        gu_ref, gt_hbm, gqkv_hbm, dbu_ref, sm2_ref, grad_ref, low_ref, sm1_ref,
        acc, a_ref, wo_ref, x_ref, ga_ref, gt_ref, gc_ref, gqkv_ref, gn_ref, sems, sems_out, _,
    ) = refs[-20:]
    j = pl.program_id(0)
    s, d = g_ref.shape
    lanes = q_ref.shape[1]
    groups = d // lanes
    last = pl.num_programs(0) - 1
    reads = (
        pltpu.make_async_copy(a_hbm.at[at_ref[0]], a_ref, sems.at[0]),
        pltpu.make_async_copy(w_hbm.at[:, pl.ds(3 * d, d)], wo_ref, sems.at[1]),
        pltpu.make_async_copy(x_hbm.at[at_ref[0]], x_ref, sems.at[2]),
    )
    writes = (
        pltpu.make_async_copy(gt_ref, gt_hbm.at[slot], sems_out.at[0]),
        pltpu.make_async_copy(gqkv_ref, gqkv_hbm.at[slot], sems_out.at[1]),
    )

    @pl.when(j == 0)
    def _():
        for copy in reads:
            copy.start()

    @pl.when(j < owners)
    def _():
        gh = jnp.concatenate([nt(g_ref[...], block[...]) for block in blocks], axis=1)
        gu = (gh * gp_ref[...].astype(F32)).astype(BF16)
        gu_ref[...] = gu
        dbu_ref[...] = col_sum(gu)
        part = nt(gu, wu_ref[...])

        @pl.when(j == 0)
        def _():
            acc[...] = part

        @pl.when(j > 0)
        def _():
            acc[...] += part

    @pl.when(j == owners - 1)
    def _():
        for copy in reads:
            copy.wait()
        gn = acc[...]
        u, r = unit(a_ref[...])
        g = g_ref[...].astype(F32)
        ga = g + norm_back(gn, u, r, gain2_ref[...].astype(F32))
        ga_ref[...] = ga
        gt = ga.astype(BF16)
        gt_ref[...] = gt
        writes[0].start()
        gc_ref[...] = nt(gt, wo_ref[...]).astype(BF16)
        sm2_ref[0:1, :] = col_sum(gn * u)
        sm2_ref[1:2, :] = col_sum(gn)
        sm2_ref[2:3, :] = col_sum(g)
        sm2_ref[3:4, :] = col_sum(gt)

    @pl.when((j >= owners) & (j < owners + groups))
    def _():
        group = j - owners
        count = lanes // HEAD_DIM
        first_head = lax.rem(group, l_ref.shape[0] // count) * count
        logs = [l_ref[pl.ds(first_head + h, 1), :] for h in range(count)]
        do = gc_ref[:, pl.ds(pl.multiple_of(group * lanes, lanes), lanes)]
        grads = attend_back(q_ref[...], k_ref[...], v_ref[...], do, logs)
        for part, grad in enumerate(grads):
            first = pl.multiple_of(part * d + group * lanes, lanes)
            gqkv_ref[:, pl.ds(first, lanes)] = grad.T

    @pl.when(j >= owners + groups)
    def _():
        part = j - owners - groups
        columns = gqkv_ref[:, pl.ds(pl.multiple_of(part * d, d), d)]
        product = nt(columns, wq_ref[...])

        @pl.when(part == 0)
        def _():
            writes[1].start()
            gn_ref[...] = product
            sm1_ref[2:3, :] = col_sum(columns)

        @pl.when(part > 0)
        def _():
            gn_ref[...] += product

        @pl.when(j == last)
        def _():
            sm1_ref[3:4, :] = col_sum(columns)
            gn = gn_ref[...]
            u, r = unit(x_ref[...].astype(F32))
            out = ga_ref[...] + norm_back(gn, u, r, gain1_ref[...].astype(F32))
            grad_ref[...] = out
            low_ref[...] = out.astype(BF16)
            sm1_ref[0:1, :] = col_sum(gn * u)
            sm1_ref[1:2, :] = col_sum(gn)
            for copy in writes:
                copy.wait()


def back(at, g, w, kept, gain1, gain2, slot, slots, owners, prev):
    xb, _, qkv, _, logs, after, _, _, gp = kept
    s, d = g.shape
    n = gp.shape[2]
    t = n // owners
    lanes = BACK_HEADS * HEAD_DIM
    groups = d // lanes
    ratio = FORWARD_HEADS // BACK_HEADS
    anywhere = pl.BlockSpec(memory_space=pl.ANY)

    def owner(j):
        return jnp.minimum(j, owners - 1)

    def group(j):
        return jnp.clip(j - owners, 0, groups - 1)

    def heads(part):
        return spec((None, s, lanes), lambda j, r: (r[0], 0, group(j) + part * groups))

    def down_block(k):
        return (w, spec((d // owners, d), lambda j, r: (owner(j), 8 + k)))

    return call(
        partial(back_kernel, slot, owners),
        "back",
        (owners + groups + 3,),
        [
            (g, fixed((s, d))),
            (gp, spec((None, s, t), lambda j, r: (r[0], 0, owner(j)))),
            (w, spec((d, t), lambda j, r: (0, 4 * d // t + owner(j)))),
            (gain2, fixed((1, d))),
            (gain1, fixed((1, d))),
            (qkv, heads(0)),
            (qkv, heads(1)),
            (qkv, heads(2)),
            (
                logs,
                spec(
                    (None, None, FORWARD_HEADS, s), lambda j, r: (r[0], group(j) // ratio, 0, 0)
                ),
            ),
            (w, spec((d, d), lambda j, r: (0, jnp.clip(j - owners - groups, 0, 2)))),
            (after, anywhere),
            (w, anywhere),
            (xb, anywhere),
        ]
        + [down_block(k) for k in range(n // d)],
        [
            ((slots, s, n), BF16, spec((None, s, t), lambda j, r: (slot, 0, owner(j)))),
            ((slots, s, d), BF16, anywhere),
            ((slots, s, 3 * d), BF16, anywhere),
            ((slots, 1, n), F32, spec((None, 1, t), lambda j, r: (slot, 0, owner(j)))),
            ((slots, 4, d), F32, fixed((None, 4, d), (slot, 0, 0))),
            ((s, d), F32, fixed((s, d))),
            ((s, d), BF16, fixed((s, d))),
            ((slots, 4, d), F32, fixed((None, 4, d), (slot, 0, 0))),
        ],
        scratch=[
            pltpu.VMEM((s, d), F32),
            pltpu.VMEM((s, d), F32),
            pltpu.VMEM((d, d), BF16),
            pltpu.VMEM((s, d), BF16),
            pltpu.VMEM((s, d), F32),
            pltpu.VMEM((s, d), BF16),
            pltpu.VMEM((s, d), BF16),
            pltpu.VMEM((s, 3 * d), BF16),
            pltpu.VMEM((s, d), F32),
            pltpu.SemaphoreType.DMA((3,)),
            pltpu.SemaphoreType.DMA((2,)),
            pltpu.VMEM((8, 128), F32),
        ],
        scalars=at,
        prev=prev,
        flops=4 * s * d * n + 8 * s * d * d + 30 * s * s * d,
    )


def weight_grad_kernel(at_ref, a_ref, b0_ref, b1_ref, send_ref, keep_ref, left, right):
    s = b0_ref.shape[0]
    step = right.shape[0] // 2
    i = pl.program_id(0)

    @pl.when(i == 0)
    def _():
        right[...] = jnp.zeros_like(right)
        left[...] = jnp.zeros_like(left)
        for image in range(2):
            left[:, image * step : image * step + s] = a_ref[image].T

    right[0:s, :] = b0_ref[...]
    right[step : step + s, :] = b1_ref[...]
    owners, rows, cols = send_ref.shape
    out = nn(left[...], right[...]).astype(BF16).reshape(owners, rows, cols)

    @pl.when(i < pl.num_programs(0) // 2)
    def _():
        send_ref[...] = out

    @pl.when(i >= pl.num_programs(0) // 2)
    def _():
        keep_ref[...] = out


def weight_grad(at, left, right, owners, replicas, name, wait=()):
    _, s, m = left.shape
    n = right.shape[2]
    chips = replicas // CORES
    rows, cols = m // owners, n // replicas
    step = -(-s // 128) * 128

    def col(image):
        def index(i, r):
            core = jnp.where(i < chips, 1 - r[2], r[2])
            return (r[1] + image, 0, lax.rem(i, chips) * CORES + core)

        return spec((None, s, cols), index)

    def out(first):
        return (
            (chips, owners, rows, cols),
            BF16,
            spec(
                (None, owners, rows, cols),
                lambda i, r: (jnp.clip(i - first, 0, chips - 1), 0, 0, 0),
            ),
        )

    return call(
        weight_grad_kernel,
        name,
        (replicas,),
        [
            (left, spec((2, s, m), lambda i, r: (r[0], 0, 0))),
            (right, col(0)),
            (right, col(1)),
        ],
        [out(0), out(chips)],
        scratch=[pltpu.VMEM((m, 2 * step), BF16), pltpu.VMEM((2 * step, cols), BF16)],
        scalars=at,
        wait=wait,
        flops=4 * s * m * n,
    )


class Place:
    def __init__(self):
        self.owners = lax.axis_size("shard")
        self.replicas = lax.axis_size("rep")
        self.chips = self.replicas // CORES
        self.z = lax.axis_index("shard")
        rep = lax.axis_index("rep")
        self.rep = rep
        self.y = rep // CORES
        self.core = rep % CORES

    def ring_z(self, block, step=1):
        n = self.owners
        return lax.ppermute(block, "shard", [(i, (i + step) % n) for i in range(n)])

    def ring_y(self, block):
        n = self.chips
        route = [
            (y * CORES + c, ((y + 1) % n) * CORES + c) for y in range(n) for c in range(CORES)
        ]
        return lax.ppermute(block, "rep", route)

    def swap_core(self, block):
        route = [(i, i ^ 1) for i in range(self.replicas)]
        return lax.ppermute(block, "rep", route)


def gather_vector(place, vector):
    held = [vector] + [place.ring_z(vector, step) for step in range(1, place.owners)]
    order = lax.rem(place.z - jnp.arange(place.owners) + place.owners, place.owners)
    return jnp.take(jnp.stack(held), order, axis=0)


def zero_after(value):
    corner = lax.slice(value, (0,) * value.ndim, (1,) * value.ndim)
    return (corner.reshape(()).astype(F32) * 0.0).astype(jnp.int32)


def gather_weights(place, w_qkv, w_out, w_up, w_down):
    rows, d = w_out.shape
    part = rows // place.replicas
    first = place.rep * part
    blocks = [w_down[k : k + rows] for k in range(0, w_down.shape[0], rows)]
    whole = jnp.concatenate([w_qkv, w_out, w_up] + blocks, axis=1)
    mine = lax.dynamic_slice_in_dim(whole, first, part, 0)
    return lax.all_gather(mine, ("shard", "rep"), axis=0, tiled=True)


def add(*terms):
    total = terms[0].astype(F32)
    for term in terms[1:]:
        total = total + term.astype(F32)
    return total.astype(BF16)


def pick(holder, index, axis):
    return lax.dynamic_index_in_dim(holder, index, axis, keepdims=False)


def finish_kernel(count, at_ref, *refs):
    pieces, out_ref = refs[:count], refs[-1]
    for i, piece in enumerate(pieces):
        cols = piece.shape[1]
        first = pl.multiple_of(at_ref[i] * cols, cols)
        out_ref[:, pl.ds(first, cols)] = piece[...].astype(F32)


def finish(pieces, parts, wait=()):
    rows, cols = pieces[0].shape
    whole = pl.BlockSpec(memory_space=pltpu.VMEM)
    out = pl.pallas_call(
        partial(finish_kernel, len(pieces)),
        in_specs=[pl.BlockSpec(memory_space=pltpu.SMEM)]
        + [whole] * len(pieces)
        + [pl.BlockSpec(memory_space=pl.ANY)] * len(wait),
        out_specs=whole,
        out_shape=jax.ShapeDtypeStruct((rows, cols * len(pieces)), F32),
        compiler_params=pltpu.CompilerParams(vmem_limit_bytes=VMEM_BYTES),
        cost_estimate=pl.CostEstimate(
            flops=0, bytes_accessed=0, transcendentals=0
        ),
        name="finish",
    )(jnp.stack(parts).astype(jnp.int32), *pieces, *wait)
    return out[None]


def reduce_chips(place, held, *earlier):
    chips = place.chips
    late = [zero_after(value) for value in earlier]
    total = pick(held, lax.rem(place.y + chips - 1, chips), 0)
    for step in range(1, chips):
        total = add(
            place.ring_y(total),
            pick(held, lax.rem(place.y + 2 * chips - 1 - step, chips), 0),
            *late,
        )
    return total


def reduce_rows(place, held, *wait):
    total = lax.psum_scatter(held, "shard", scatter_dimension=0, tiled=True)[0]
    chips = place.chips
    pieces, parts = [], []
    for t in range(chips):
        if t > 0:
            total = place.ring_y(total)
        chip = lax.rem(place.y - t + chips, chips)
        pieces += [total, place.swap_core(total)]
        parts += [chip * CORES + place.core, chip * CORES + 1 - place.core]
    return finish(pieces, parts, wait)


def sum_small(place, table):
    total = table + place.swap_core(table)
    ring = total
    for _ in range(1, place.chips):
        ring = place.ring_y(ring)
        total = total + ring
    owners = place.owners
    out = pick(total, place.z, 0)
    for step in range(1, owners):
        out = out + place.ring_z(pick(total, lax.rem(place.z + step, owners), 0), step)
    return out[None]


def per_device(
    images, cotangent, ln1_scale, ln1_shift, w_qkv, bias_qv, w_out, bias_out,
    ln2_scale, ln2_shift, w_up, bias_up, w_down, bias_down,
):
    place = Place()
    section = lax.axis_index("section")
    first = section == 0
    _, s, d = images.shape

    given = (
        ln1_scale, ln1_shift, bias_qv, bias_out, ln2_scale, ln2_shift, bias_up, bias_down
    )
    widths = [v.shape[1] for v in given]
    packed = gather_vector(place, jnp.concatenate(given, axis=1)[0])
    w = gather_weights(place, w_qkv[0], w_out[0], w_up[0], w_down[0])

    whole = []
    start = 0
    for width in widths:
        whole.append(packed[:, start : start + width].reshape(1, -1))
        start += width
    gain1, shift1, bias_two, bias_o, gain2, shift2, bias_u, bias_d = whole
    bias_mixed = jnp.concatenate(
        [bias_two[:, :d], jnp.zeros((1, d), BF16), bias_two[:, d:]], axis=1
    )
    slots = 4

    def send_on(block):
        return lax.ppermute(block, "section", [(0, 1)])

    def send_back(block):
        return lax.ppermute(block, "section", [(1, 0)])

    vectors = (gain1, shift1, bias_mixed, bias_o, gain2, shift2, bias_u, bias_d)
    kept = (None,) * 9

    def forward(x, slot, with_down):
        nonlocal kept
        results = front(x, w, vectors, slot, slots, place.owners, kept, with_down)
        kept = tuple(results[:9])
        return results[9] if with_down else None

    def forward_down(slot, *earlier):
        return down(hidden, w, after, bias_d, slot, place.owners, earlier)

    gslots = 3
    gu = gt = gqkv = dbu = sm2 = sm1 = None

    def back_mlp(source, upstream, slot, *wait):
        nonlocal gu, gt, dbu, sm2
        gu, ga, gt, gc, dbu, sm2 = mlp_back(
            source, upstream, gp, w, after, gain2, slot, gslots, place.owners,
            (gu, None, gt, None, dbu, sm2), wait,
        )
        return ga, gc

    def back_attn(source, gc, slot, *wait):
        nonlocal gqkv
        gqkv = attn_back(source, qkv, gc, logs, slot, gslots, (gqkv,), wait)

    def back_qkv(source, ga, slot, *wait):
        nonlocal sm1
        grad, low, sm1 = qkv_back(source, gqkv, w, xb, ga, gain1, slot, (None, None, sm1), wait)
        return grad, low

    def back_all(source, upstream, slot):
        nonlocal gu, gt, gqkv, dbu, sm2, sm1
        gu, gt, gqkv, dbu, sm2, grad, low, sm1 = back(
            source, upstream, w, kept, gain1, gain2, slot, gslots, place.owners,
            (gu, gt, gqkv, dbu, sm2, None, None, sm1),
        )
        return grad, low

    def source_slot(value):
        return jnp.asarray(value, jnp.int32).reshape(1)

    out0 = forward(images[0], 0, True)
    arrived0 = send_on(out0)
    out1 = forward(images[1], 1, True)
    arrived1 = send_on(out1)
    forward(arrived0, 2, False)
    xb, n1, qkv, ctx, logs, after, n2, hidden, gp = kept
    source = source_slot(2)
    up0 = cotangent[0]
    grad0, low0 = back_all(source, up0, 0)
    returned0 = send_back(low0)

    forward(arrived1, 3, False)
    xb, n1, qkv, ctx, logs, after, n2, hidden, gp = kept
    source = source_slot(jnp.where(first, 0, 3))
    up1 = jnp.where(first, returned0, cotangent[1])
    grad1, low1 = back_all(source, up1, 1)
    up2 = send_back(low1)

    out2 = forward_down(2, low1)
    out3 = forward_down(3, out2)
    section_out = jnp.where(first, jnp.stack([out0, out1]), jnp.stack([out2, out3]))
    at = jnp.stack([section, 1 - section, place.core]).astype(jnp.int32)

    sizes = (place.owners, place.replicas)

    def products(left, right, name, *earlier):
        sent, kept = weight_grad(at, left, right, *sizes, name, earlier)
        return add(kept, place.swap_core(sent))

    source = source_slot(1)
    h_down = products(hidden, jnp.stack([up0, up1, up2]), "dw_down", out2, out3)
    t_down = reduce_chips(place, h_down)
    ga, gc = back_mlp(source, up2, 2, h_down)
    h_up = products(n2, gu, "dw_up")
    t_up = reduce_chips(place, h_up)
    h_out = products(ctx, gt, "dw_out", t_down)
    t_out = reduce_chips(place, h_out)
    back_attn(source, gc, 2, h_out, h_up)
    h_qkv = products(n1, gqkv, "dw_qkv")
    t_qkv = reduce_chips(place, h_qkv)
    grad2, low2 = back_qkv(source, ga, 2, h_qkv, t_up)

    grad_in = jnp.where(
        first,
        jnp.stack([grad1, grad2]),
        jnp.stack([low0.astype(F32), low1.astype(F32)]),
    )
    gw_down = reduce_rows(place, t_down)
    gw_up = reduce_rows(place, t_up)
    gw_out = reduce_rows(place, t_out)
    gw_qkv = reduce_rows(place, t_qkv, gw_down, gw_up, gw_out, grad_in, section_out)

    def own(holder):
        pair = lax.dynamic_slice_in_dim(holder, 1 - section, 2, 0)
        return jnp.sum(pair, axis=0)

    sm1, sm2, dbu = own(sm1), own(sm2), own(dbu)
    smalls = (
        sm1[0:1], sm1[1:2], jnp.concatenate([sm1[2:3], sm1[3:4]], axis=1), sm2[3:4],
        sm2[0:1], sm2[1:2], dbu, sm2[2:3],
    )
    table = jnp.concatenate([v.reshape(place.owners, -1) for v in smalls], axis=1)
    mine = sum_small(place, table)
    shares = []
    start = 0
    for width in widths:
        shares.append(mine[:, start : start + width])
        start += width
    (g_ln1s, g_ln1b, g_bqv, g_bo, g_ln2s, g_ln2b, g_bu, g_bd) = shares
    return (
        section_out[None], grad_in[None], g_ln1s, g_ln1b, gw_qkv, g_bqv, gw_out, g_bo,
        g_ln2s, g_ln2b, gw_up, g_bu, gw_down, g_bd,
    )


def solution(mesh):
    batch = P(("shard", "rep"), None, None)
    layers = P("section", ("shard", "rep"), None, None)
    vec = P("section", "shard")
    mat = P("section", "shard", None)
    in_specs = (
        batch, batch, vec, vec, mat, vec, mat, vec, vec, vec, mat, vec, mat, vec
    )
    out_specs = (
        layers, layers, vec, vec, mat, vec, mat, vec, vec, vec, mat, vec, mat, vec
    )
    return jax.shard_map(
        per_device, mesh=mesh, in_specs=in_specs, out_specs=out_specs, check_vma=False
    )
```
